256 devices in a mesh: tm: 64 (over x, y_lo, z), gz: 4 (over y_hi, core).
Axes of the slice: x: 4, y: 4 (y_hi: 2, y_lo: 2; y = y_hi * 2 + y_lo), z: 8, core: 2. Of those that a mesh axis runs over, the one named last changes fastest.
Arguments:
- states: float32 [64, 3, 64, 16, 128], P('tm', None, 'gz'), may hold values from -4 to 4
- rate: float32 [64, 16, 128], P('gz'), may hold values from 0.1 to 40
Outputs:
- new_states: float32 [64, 3, 64, 16, 128], P('tm', None, 'gz')
The draws below stay inside these ranges and needn't reach their ends.
All inputs are finite; a program needn't handle non-finite values.
Results may differ from the reference program's by a relative error of at most 0.000044.
Values sent between devices are 32-bit elements; how exact they have to be, the bound alone decides.
A program may use at most 128 MiB of HBM per device.

```python
import math
import jax
import jax.numpy as jnp
from jax import lax

NX = 128
NY = 16
STEPS = 2
NZ = 64
SLICES = 64


def steps_of(key, shape, cuts, low, largest):
    gain = 1.0
    for dim, shards_of in cuts:
        steps = jax.random.uniform(jax.random.fold_in(jax.random.fold_in(key, 6), dim), (shards_of,), jnp.float32, low / len(cuts), largest / len(cuts))
        gain = gain * jnp.repeat(jnp.exp(steps), shape[dim] // shards_of).reshape((-1,) + (1,) * (len(shape) - 1 - dim))
    return gain


def gaussian(rng, extent, scale, limit, shards=(), held_as=jnp.bfloat16):
    values = jax.random.normal(rng, extent, jnp.float32) * scale
    if len(shards) > 0:
        values = steps_of(rng, extent, shards, -0.22, 0.18) * values
    return jnp.clip(values, min=-limit, max=limit).astype(held_as)


def setup_inputs(seed: int = 0) -> dict:
    key_of = jax.random.split(jax.random.key(seed), 3)
    states = gaussian(key_of[0], (SLICES, 3, NZ, NY, NX), 0.5, 4.0, ((0, 64), (2, 4)), jnp.float32)
    rate = jnp.clip(jnp.exp(math.log(40.0) - 5.9914645 * jax.random.uniform(key_of[1], (NZ, NY, NX), jnp.float32) ** steps_of(key_of[1], (NZ, NY, NX), ((0, 4),), -0.2, 0.2)), 0.1, 40.0)
    return dict(states=states, rate=rate)


VISCOSITY = 0.05
TIME_STEP = 0.2


def tendency(padded):
    core = padded[:, 1:-1]
    along_x = (jnp.roll(core, -1, 3) - jnp.roll(core, 1, 3)) * 0.5
    along_y = (jnp.roll(core, -1, 2) - jnp.roll(core, 1, 2)) * 0.5
    along_z = (padded[:, 2:] - padded[:, :-2]) * 0.5
    spread = jnp.roll(core, -1, 3) + jnp.roll(core, 1, 3) + jnp.roll(core, -1, 2) + jnp.roll(core, 1, 2)
    spread = spread + padded[:, 2:] + padded[:, :-2] - 6.0 * core
    advect = core[0:1] * along_x + core[1:2] * along_y + core[2:3] * along_z
    return -advect + VISCOSITY * spread


def rate_of(field):
    return tendency(jnp.pad(field, ((0, 0), (1, 1), (0, 0), (0, 0)), mode="wrap"))


def fine(field):
    for step in range(STEPS):
        first = field + TIME_STEP * rate_of(field)
        second = 0.75 * field + 0.25 * (first + TIME_STEP * rate_of(first))
        field = (1.0 / 3.0) * field + (2.0 / 3.0) * (second + TIME_STEP * rate_of(second))
    return field


def reference(states, rate):
    damp = jnp.exp(-rate / SLICES).astype(jnp.float32)

    def slice_jump(field):
        return fine(field) - damp * field

    jumps = lax.map(slice_jump, states)

    def chain(carry, jump):
        nexts = damp * carry + jump
        return nexts, nexts

    _, later = lax.scan(chain, states[0], jumps[:-1])
    return jnp.concatenate([states[0:1], later], 0)
```

```python
import jax
import jax.numpy as jnp
from jax import lax
from jax.experimental import pallas as pl
from jax.experimental.pallas import tpu as pltpu
from jax.sharding import PartitionSpec as P

STEPS = 2
VISCOSITY = 0.05
TIME_STEP = 0.2
SLICES = 64
RING = 8
ROWS = 8
SLABS = 4
WIDE = 3 * STEPS
OWN = 16
SPAN = OWN + 2 * WIDE
GROUPS = 4
MESH = pl.DeviceIdType.MESH

KEEP = 1.0 - 6.0 * VISCOSITY * TIME_STEP
NEAR = VISCOSITY * TIME_STEP
HALF = 0.5 * TIME_STEP
WEIGHTS = ((0.0, 1.0), (0.75, 0.25), (1.0 / 3.0, 2.0 / 3.0))


def stage_plane(kind, src, base, plane, put):
    old, new = WEIGHTS[kind]
    row = lax.broadcasted_iota(jnp.int32, (8, 128), 0)
    first, last = row == 0, row == 7
    tile = 2 * plane
    core = [[src[c, tile + h] for h in range(2)] for c in range(3)]
    wind = [[core[c][h] * (new * HALF) for h in range(2)] for c in range(3)]
    for c in range(3):
        a, b = core[c]
        ra, rb = pltpu.roll(a, 1, 0), pltpu.roll(b, 1, 0)
        la, lb = pltpu.roll(a, 7, 0), pltpu.roll(b, 7, 0)
        before = (jnp.where(first, rb, ra), jnp.where(first, ra, rb))
        after = (jnp.where(last, lb, la), jnp.where(last, la, lb))
        for h in range(2):
            v = core[c][h]
            xm, xp = pltpu.roll(v, 1, 1), pltpu.roll(v, 127, 1)
            zm, zp = src[c, tile + h - 2], src[c, tile + h + 2]
            near = (xp + xm) + (after[h] + before[h]) + (zp + zm)
            advect = wind[0][h] * (xp - xm) + wind[1][h] * (after[h] - before[h]) + wind[2][h] * (zp - zm)
            out = (new * KEEP) * v + ((new * NEAR) * near - advect)
            if kind:
                out = out + old * base[c, tile + h]
            put(c, h, out)


def kernel(states, rate, out, w0, w1, w2, w3, w4, w5, jump, got, total, tots, path,
           load_sem, halo_send, halo_recv, up_send, up_recv, row_send, row_recv, down_send, down_recv, own_sem):
    tm, gz = lax.axis_index("tm"), lax.axis_index("gz")
    zi, row = lax.rem(tm, RING), lax.div(tm, RING)
    above, below = lax.rem(gz + 1, SLABS), lax.rem(gz + SLABS - 1, SLABS)
    far = lax.rem(gz, 2)
    start = row * RING

    barrier = pltpu.get_barrier_semaphore()
    for peer in (above, below):
        pl.semaphore_signal(barrier, inc=1, device_id={"gz": peer}, device_id_type=MESH)
    for q in range(1, RING):
        pl.semaphore_signal(barrier, inc=1, device_id={"tm": start + lax.rem(zi + q, RING)}, device_id_type=MESH)

    def greet(q, carry):
        pl.semaphore_signal(barrier, inc=1, device_id={"tm": q * RING + zi}, device_id_type=MESH)
        return carry

    lax.fori_loop(0, row, greet, 0)
    load = pltpu.make_async_copy(states, w0.at[:, pl.ds(2 * WIDE, 2 * OWN)], load_sem)
    load.start()
    pl.semaphore_wait(barrier, 2 + (RING - 1) + (ROWS - 1 - row))

    down_halo = pltpu.make_async_remote_copy(
        states.at[:, pl.ds(0, 2 * WIDE)], w0.at[:, pl.ds(2 * (OWN + WIDE), 2 * WIDE)], halo_send.at[0], halo_recv.at[1],
        device_id={"gz": below}, device_id_type=MESH)
    up_halo = pltpu.make_async_remote_copy(
        states.at[:, pl.ds(2 * (OWN - WIDE), 2 * WIDE)], w0.at[:, pl.ds(0, 2 * WIDE)], halo_send.at[1], halo_recv.at[0],
        device_id={"gz": above}, device_id_type=MESH)
    down_halo.start()
    up_halo.start()

    @pl.when(tm == 0)
    def _():
        pltpu.make_async_copy(states, out, own_sem.at[0]).start()

    works = (w0, w1, w2, w3, w4, w5)
    keep_own = jnp.where(tm == 0, 0.0, 1.0)

    def stages(first_plane, count, shift):
        for k in range(1, 2 * 3 + 1):
            src, base = works[k - 1], works[3 * ((k - 1) // 3)]
            kind = (k - 1) % 3
            begin = first_plane(k)

            def plane_turn(i, carry, k=k, src=src, base=base, kind=kind, begin=begin):
                plane = begin + i
                if k < 6:
                    def put(c, h, value):
                        works[k][c, 2 * plane + h] = value
                else:
                    damp = [jnp.exp(rate[2 * (plane - WIDE) + h] * (-1.0 / SLICES)) * keep_own for h in range(2)]

                    def put(c, h, value):
                        jump[c, 2 * (plane - WIDE) + h] = value - damp[h] * w0[c, 2 * plane + h]

                stage_plane(kind, src, base, plane, put)
                return carry

            lax.fori_loop(0, count(k), plane_turn, 0)

    bases = (6, 10 - 8 * far, 2 + 8 * far)

    def tile_of(group, k):
        if group < 3:
            return 2 * bases[group] + k
        return k + jnp.where(k >= 4, 24, 0)

    def send_up(group):
        for q in (4, 3, 5, 2, 6, 1, 7):
            peer = lax.rem(zi + q, RING)
            pltpu.make_async_remote_copy(
                jump.at[:, tile_of(group, peer)], got.at[group, zi], up_send.at[group], up_recv.at[group],
                device_id={"tm": start + peer}, device_id_type=MESH).start()

    def all_of(buf, send, recv):
        return pltpu.make_async_remote_copy(
            buf.at[pl.ds(0, RING - 1)], buf.at[pl.ds(0, RING - 1)], send, recv,
            device_id={"tm": tm}, device_id_type=MESH)

    def damp_of(group):
        return jnp.exp(rate[tile_of(group, zi)] * (-1.0 / SLICES))

    def sum_row(group):
        all_of(got.at[group], up_send.at[group], up_recv.at[group]).wait_recv()
        mine = tile_of(group, zi)
        for c in range(3):
            got[group, zi, c] = jump[c, mine]
        damp = damp_of(group)
        acc = [got[group, 0, c] for c in range(3)]
        for z in range(1, RING):
            acc = [damp * acc[c] + got[group, z, c] for c in range(3)]
        for c in range(3):
            total[group, c] = acc[c]

        def tell(later, carry):
            pltpu.make_async_remote_copy(
                total.at[group], tots.at[group, row], row_send.at[group, later], row_recv.at[group, row],
                device_id={"tm": later * RING + zi}, device_id_type=MESH).start()
            return carry

        lax.fori_loop(row + 1, ROWS, tell, 0)

    def send_down(group):
        damp = damp_of(group)
        eighth = damp * damp
        eighth = eighth * eighth
        eighth = eighth * eighth

        def add(q, carry):
            pltpu.make_async_remote_copy(
                total.at[group], tots.at[group, q], row_send.at[group, q], row_recv.at[group, q],
                device_id={"tm": q * RING + zi}, device_id_type=MESH).wait_recv()
            return tuple(eighth * carry[c] + tots[group, q, c] for c in range(3))

        acc = lax.fori_loop(0, row, add, tuple(jnp.zeros((8, 128), jnp.float32) for _ in range(3)))
        for z in range(RING):
            for c in range(3):
                path[group, z, c] = acc[c]
            if z < RING - 1:
                acc = [damp * acc[c] + got[group, z, c] for c in range(3)]
        mine = tile_of(group, zi)
        for q in (4, 3, 5, 2, 6, 1, 7):
            peer = lax.rem(zi + q, RING)

            @pl.when(start + peer > 0)
            def _():
                pltpu.make_async_remote_copy(
                    path.at[group, peer], out.at[:, mine], down_send.at[group, q], down_recv.at[group, q],
                    device_id={"tm": start + peer}, device_id_type=MESH).start()

        @pl.when(tm > 0)
        def _():
            pltpu.make_async_copy(path.at[group, zi], out.at[:, mine], own_sem.at[group]).start()

    load.wait()
    stages(lambda k: WIDE + k, lambda k: OWN - 2 * k, 0)
    send_up(0)

    def side(upper):
        @pl.when(upper == 0)
        def _():
            up_halo.wait_recv()

        @pl.when(upper == 1)
        def _():
            down_halo.wait_recv()

        stages(lambda k: jnp.where(upper == 1, OWN + WIDE - k, k), lambda k: WIDE, 0)

    side(1 - far)
    send_up(1)
    side(far)
    send_up(2)
    send_up(3)
    sum_row(0)
    sum_row(1)
    send_down(0)
    sum_row(2)
    send_down(1)
    sum_row(3)
    send_down(2)
    send_down(3)

    for group in range(GROUPS):
        mine = tile_of(group, zi)
        all_of(got.at[group], up_send.at[group], up_recv.at[group]).wait_send()

        def told(later, carry, group=group):
            pltpu.make_async_remote_copy(
                total.at[group], tots.at[group, row], row_send.at[group, later], row_recv.at[group, row],
                device_id={"tm": later * RING + zi}, device_id_type=MESH).wait_send()
            return carry

        lax.fori_loop(row + 1, ROWS, told, 0)
        for q in range(1, RING):
            peer, source = lax.rem(zi + q, RING), lax.rem(zi + RING - q, RING)

            @pl.when(start + peer > 0)
            def _():
                pltpu.make_async_remote_copy(
                    path.at[group, peer], out.at[:, mine], down_send.at[group, q], down_recv.at[group, q],
                    device_id={"tm": start + peer}, device_id_type=MESH).wait_send()

            @pl.when(tm > 0)
            def _():
                pltpu.make_async_remote_copy(
                    path.at[group, zi], out.at[:, tile_of(group, source)], down_send.at[group, q], down_recv.at[group, q],
                    device_id={"tm": start + source}, device_id_type=MESH).wait_recv()

        @pl.when(tm > 0)
        def _():
            pltpu.make_async_copy(path.at[group, zi], out.at[:, mine], own_sem.at[group]).wait()

    @pl.when(tm == 0)
    def _():
        pltpu.make_async_copy(states, out, own_sem.at[0]).wait()

    down_halo.wait_send()
    up_halo.wait_send()


def shards(states, rate):
    f32 = jnp.float32
    work = pltpu.VMEM((3, 2 * SPAN, 8, 128), f32)
    dma = pltpu.SemaphoreType.DMA
    out = pl.pallas_call(
        kernel,
        out_shape=jax.ShapeDtypeStruct((3, 2 * OWN, 8, 128), f32),
        in_specs=[pl.BlockSpec(memory_space=pl.ANY), pl.BlockSpec(memory_space=pltpu.VMEM)],
        out_specs=pl.BlockSpec(memory_space=pl.ANY),
        scratch_shapes=[work] * 6 + [
            pltpu.VMEM((3, 2 * OWN, 8, 128), f32),
            pltpu.VMEM((GROUPS, RING, 3, 8, 128), f32),
            pltpu.VMEM((GROUPS, 3, 8, 128), f32),
            pltpu.VMEM((GROUPS, ROWS, 3, 8, 128), f32),
            pltpu.VMEM((GROUPS, RING, 3, 8, 128), f32),
            dma, dma((2,)), dma((2,)), dma((GROUPS,)), dma((GROUPS,)),
            dma((GROUPS, ROWS)), dma((GROUPS, ROWS)), dma((GROUPS, RING)), dma((GROUPS, RING)), dma((GROUPS,)),
        ],
        compiler_params=pltpu.CompilerParams(collective_id=0, has_side_effects=True, vmem_limit_bytes=32 * 1024 * 1024),
    )(states.reshape(3, 2 * OWN, 8, 128), rate.reshape(2 * OWN, 8, 128))
    return out.reshape(1, 3, OWN, 16, 128)


def solution(mesh):
    return jax.shard_map(
        shards,
        mesh=mesh,
        in_specs=(P("tm", None, "gz", None, None), P("gz", None, None)),
        out_specs=P("tm", None, "gz", None, None),
        check_vma=False,
    )
```

```python
import jax
import jax.numpy as jnp
from jax import lax
from jax.experimental import pallas as pl
from jax.experimental.pallas import tpu as pltpu
from jax.sharding import PartitionSpec as P

STEPS = 2
VISCOSITY = 0.05
TIME_STEP = 0.2
SLICES = 64
RING = 8
ROWS = 8
SLABS = 4
WIDE = 3 * STEPS
OWN = 16
SPAN = OWN + 2 * WIDE
GROUPS = 4
MESH = pl.DeviceIdType.MESH

KEEP = 1.0 - 6.0 * VISCOSITY * TIME_STEP
NEAR = VISCOSITY * TIME_STEP
HALF = 0.5 * TIME_STEP
WEIGHTS = ((0.0, 1.0), (0.75, 0.25), (1.0 / 3.0, 2.0 / 3.0))


def stage_plane(kind, src, base, plane, put):
    old, new = WEIGHTS[kind]
    row = lax.broadcasted_iota(jnp.int32, (8, 128), 0)
    first, last = row == 0, row == 7
    tile = 2 * plane
    core = [[src[c, tile + h] for h in range(2)] for c in range(3)]
    wind = [[core[c][h] * (new * HALF) for h in range(2)] for c in range(3)]
    for c in range(3):
        a, b = core[c]
        ra, rb = pltpu.roll(a, 1, 0), pltpu.roll(b, 1, 0)
        la, lb = pltpu.roll(a, 7, 0), pltpu.roll(b, 7, 0)
        before = (jnp.where(first, rb, ra), jnp.where(first, ra, rb))
        after = (jnp.where(last, lb, la), jnp.where(last, la, lb))
        for h in range(2):
            v = core[c][h]
            xm, xp = pltpu.roll(v, 1, 1), pltpu.roll(v, 127, 1)
            zm, zp = src[c, tile + h - 2], src[c, tile + h + 2]
            near = (xp + xm) + (after[h] + before[h]) + (zp + zm)
            advect = wind[0][h] * (xp - xm) + wind[1][h] * (after[h] - before[h]) + wind[2][h] * (zp - zm)
            out = (new * KEEP) * v + ((new * NEAR) * near - advect)
            if kind:
                out = out + old * base[c, tile + h]
            put(c, h, out)


def kernel(states, rate_in, out, rate, w0, w1, w2, w3, w4, w5, jump, got, total, tots, path,
           load_sem, halo_send, halo_recv, up_send, up_recv, row_send, row_recv, down_send, down_recv, own_sem):
    tm, gz = lax.axis_index("tm"), lax.axis_index("gz")
    zi, row = lax.rem(tm, RING), lax.div(tm, RING)
    above, below = lax.rem(gz + 1, SLABS), lax.rem(gz + SLABS - 1, SLABS)
    far = lax.rem(gz, 2)
    start = row * RING

    load = pltpu.make_async_copy(states, w0.at[:, pl.ds(2 * WIDE, 2 * OWN)], load_sem.at[0])
    load.start()
    load_rate = pltpu.make_async_copy(rate_in, rate, load_sem.at[1])
    load_rate.start()
    barrier = pltpu.get_barrier_semaphore()
    for peer in (above, below):
        pl.semaphore_signal(barrier, inc=1, device_id={"gz": peer}, device_id_type=MESH)
    for q in range(1, RING):
        pl.semaphore_signal(barrier, inc=1, device_id={"tm": start + lax.rem(zi + q, RING)}, device_id_type=MESH)

    def greet(q, carry):
        pl.semaphore_signal(barrier, inc=1, device_id={"tm": q * RING + zi}, device_id_type=MESH)
        return carry

    lax.fori_loop(0, row, greet, 0)
    pl.semaphore_wait(barrier, 2 + (RING - 1) + (ROWS - 1 - row))

    down_halo = pltpu.make_async_remote_copy(
        states.at[:, pl.ds(0, 2 * WIDE)], w0.at[:, pl.ds(2 * (OWN + WIDE), 2 * WIDE)], halo_send.at[0], halo_recv.at[1],
        device_id={"gz": below}, device_id_type=MESH)
    up_halo = pltpu.make_async_remote_copy(
        states.at[:, pl.ds(2 * (OWN - WIDE), 2 * WIDE)], w0.at[:, pl.ds(0, 2 * WIDE)], halo_send.at[1], halo_recv.at[0],
        device_id={"gz": above}, device_id_type=MESH)
    down_halo.start()
    up_halo.start()

    @pl.when(tm == 0)
    def _():
        pltpu.make_async_copy(states, out, own_sem.at[0]).start()

    works = (w0, w1, w2, w3, w4, w5)
    keep_own = jnp.where(tm == 0, 0.0, 1.0)

    def stages(first_plane, count, shift):
        for k in range(1, 2 * 3 + 1):
            src, base = works[k - 1], works[3 * ((k - 1) // 3)]
            kind = (k - 1) % 3
            begin = first_plane(k)

            def plane_turn(i, carry, k=k, src=src, base=base, kind=kind, begin=begin):
                plane = begin + i
                if k < 6:
                    def put(c, h, value):
                        works[k][c, 2 * plane + h] = value
                else:
                    damp = [jnp.exp(rate[2 * (plane - WIDE) + h] * (-1.0 / SLICES)) * keep_own for h in range(2)]

                    def put(c, h, value):
                        jump[c, 2 * (plane - WIDE) + h] = value - damp[h] * w0[c, 2 * plane + h]

                stage_plane(kind, src, base, plane, put)
                return carry

            lax.fori_loop(0, count(k), plane_turn, 0)

    bases = (6, 10 - 8 * far, 2 + 8 * far)

    def tile_of(group, k):
        if group < 3:
            return 2 * bases[group] + k
        return k + jnp.where(k >= 4, 24, 0)

    def send_up(group):
        for q in (4, 3, 5, 2, 6, 1, 7):
            peer = lax.rem(zi + q, RING)
            pltpu.make_async_remote_copy(
                jump.at[:, tile_of(group, peer)], got.at[group, zi], up_send.at[group], up_recv.at[group],
                device_id={"tm": start + peer}, device_id_type=MESH).start()

    def all_of(buf, send, recv):
        return pltpu.make_async_remote_copy(
            buf.at[pl.ds(0, RING - 1)], buf.at[pl.ds(0, RING - 1)], send, recv,
            device_id={"tm": tm}, device_id_type=MESH)

    def damp_of(group):
        return jnp.exp(rate[tile_of(group, zi)] * (-1.0 / SLICES))

    def sum_row(group):
        all_of(got.at[group], up_send.at[group], up_recv.at[group]).wait_recv()
        mine = tile_of(group, zi)
        for c in range(3):
            got[group, zi, c] = jump[c, mine]
        damp = damp_of(group)
        acc = [got[group, 0, c] for c in range(3)]
        for z in range(1, RING):
            acc = [damp * acc[c] + got[group, z, c] for c in range(3)]
        for c in range(3):
            total[group, c] = acc[c]

        def tell(later, carry):
            pltpu.make_async_remote_copy(
                total.at[group], tots.at[group, row], row_send.at[group, later], row_recv.at[group, row],
                device_id={"tm": later * RING + zi}, device_id_type=MESH).start()
            return carry

        lax.fori_loop(row + 1, ROWS, tell, 0)

    def send_down(group):
        damp = damp_of(group)
        eighth = damp * damp
        eighth = eighth * eighth
        eighth = eighth * eighth

        def add(q, carry):
            pltpu.make_async_remote_copy(
                total.at[group], tots.at[group, q], row_send.at[group, q], row_recv.at[group, q],
                device_id={"tm": q * RING + zi}, device_id_type=MESH).wait_recv()
            return tuple(eighth * carry[c] + tots[group, q, c] for c in range(3))

        acc = lax.fori_loop(0, row, add, tuple(jnp.zeros((8, 128), jnp.float32) for _ in range(3)))
        for z in range(RING):
            for c in range(3):
                path[group, z, c] = acc[c]
            if z < RING - 1:
                acc = [damp * acc[c] + got[group, z, c] for c in range(3)]
        mine = tile_of(group, zi)
        for q in (4, 3, 5, 2, 6, 1, 7):
            peer = lax.rem(zi + q, RING)

            @pl.when(start + peer > 0)
            def _():
                pltpu.make_async_remote_copy(
                    path.at[group, peer], out.at[:, mine], down_send.at[group, q], down_recv.at[group, q],
                    device_id={"tm": start + peer}, device_id_type=MESH).start()

        @pl.when(tm > 0)
        def _():
            pltpu.make_async_copy(path.at[group, zi], out.at[:, mine], own_sem.at[group]).start()

    load.wait()
    load_rate.wait()
    stages(lambda k: WIDE + k, lambda k: OWN - 2 * k, 0)
    send_up(0)

    def side(upper):
        @pl.when(upper == 0)
        def _():
            up_halo.wait_recv()

        @pl.when(upper == 1)
        def _():
            down_halo.wait_recv()

        stages(lambda k: jnp.where(upper == 1, OWN + WIDE - k, k), lambda k: WIDE, 0)

    side(1 - far)
    send_up(1)
    side(far)
    send_up(2)
    send_up(3)
    sum_row(0)
    sum_row(1)
    send_down(0)
    sum_row(2)
    send_down(1)
    sum_row(3)
    send_down(2)
    send_down(3)

    for group in range(GROUPS):
        mine = tile_of(group, zi)
        all_of(got.at[group], up_send.at[group], up_recv.at[group]).wait_send()

        def told(later, carry, group=group):
            pltpu.make_async_remote_copy(
                total.at[group], tots.at[group, row], row_send.at[group, later], row_recv.at[group, row],
                device_id={"tm": later * RING + zi}, device_id_type=MESH).wait_send()
            return carry

        lax.fori_loop(row + 1, ROWS, told, 0)
        for q in range(1, RING):
            peer, source = lax.rem(zi + q, RING), lax.rem(zi + RING - q, RING)

            @pl.when(start + peer > 0)
            def _():
                pltpu.make_async_remote_copy(
                    path.at[group, peer], out.at[:, mine], down_send.at[group, q], down_recv.at[group, q],
                    device_id={"tm": start + peer}, device_id_type=MESH).wait_send()

            @pl.when(tm > 0)
            def _():
                pltpu.make_async_remote_copy(
                    path.at[group, zi], out.at[:, tile_of(group, source)], down_send.at[group, q], down_recv.at[group, q],
                    device_id={"tm": start + source}, device_id_type=MESH).wait_recv()

        @pl.when(tm > 0)
        def _():
            pltpu.make_async_copy(path.at[group, zi], out.at[:, mine], own_sem.at[group]).wait()

    @pl.when(tm == 0)
    def _():
        pltpu.make_async_copy(states, out, own_sem.at[0]).wait()

    down_halo.wait_send()
    up_halo.wait_send()


def shards(states, rate):
    f32 = jnp.float32
    work = pltpu.VMEM((3, 2 * SPAN, 8, 128), f32)
    dma = pltpu.SemaphoreType.DMA
    out = pl.pallas_call(
        kernel,
        out_shape=jax.ShapeDtypeStruct((3, 2 * OWN, 8, 128), f32),
        in_specs=[pl.BlockSpec(memory_space=pltpu.HBM), pl.BlockSpec(memory_space=pltpu.HBM)],
        out_specs=pl.BlockSpec(memory_space=pl.ANY),
        scratch_shapes=[pltpu.VMEM((2 * OWN, 8, 128), f32)] + [work] * 6 + [
            pltpu.VMEM((3, 2 * OWN, 8, 128), f32),
            pltpu.VMEM((GROUPS, RING, 3, 8, 128), f32),
            pltpu.VMEM((GROUPS, 3, 8, 128), f32),
            pltpu.VMEM((GROUPS, ROWS, 3, 8, 128), f32),
            pltpu.VMEM((GROUPS, RING, 3, 8, 128), f32),
            dma((2,)), dma((2,)), dma((2,)), dma((GROUPS,)), dma((GROUPS,)),
            dma((GROUPS, ROWS)), dma((GROUPS, ROWS)), dma((GROUPS, RING)), dma((GROUPS, RING)), dma((GROUPS,)),
        ],
        compiler_params=pltpu.CompilerParams(collective_id=0, has_side_effects=True, vmem_limit_bytes=32 * 1024 * 1024),
    )(pltpu.with_memory_space_constraint(states.reshape(3, 2 * OWN, 8, 128), pltpu.HBM), pltpu.with_memory_space_constraint(rate.reshape(2 * OWN, 8, 128), pltpu.HBM))
    return out.reshape(1, 3, OWN, 16, 128)


def solution(mesh):
    return jax.shard_map(
        shards,
        mesh=mesh,
        in_specs=(P("tm", None, "gz", None, None), P("gz", None, None)),
        out_specs=P("tm", None, "gz", None, None),
        check_vma=False,
    )
```

```python
import jax
import jax.numpy as jnp
from jax import lax
from jax.experimental import pallas as pl
from jax.experimental.pallas import tpu as pltpu
from jax.sharding import PartitionSpec as P

STEPS = 2
VISCOSITY = 0.05
TIME_STEP = 0.2
SLICES = 64
RING = 8
ROWS = 8
SLABS = 4
WIDE = 3 * STEPS
OWN = 16
SPAN = OWN + 2 * WIDE
GROUPS = 4
MESH = pl.DeviceIdType.MESH

KEEP = 1.0 - 6.0 * VISCOSITY * TIME_STEP
NEAR = VISCOSITY * TIME_STEP
HALF = 0.5 * TIME_STEP
WEIGHTS = ((0.0, 1.0), (0.75, 0.25), (1.0 / 3.0, 2.0 / 3.0))


def stage_plane(kind, src, base, plane, put):
    old, new = WEIGHTS[kind]
    row = lax.broadcasted_iota(jnp.int32, (8, 128), 0)
    first, last = row == 0, row == 7
    tile = 2 * plane
    core = [[src[c, tile + h] for h in range(2)] for c in range(3)]
    wind = [[core[c][h] * (new * HALF) for h in range(2)] for c in range(3)]
    for c in range(3):
        a, b = core[c]
        ra, rb = pltpu.roll(a, 1, 0), pltpu.roll(b, 1, 0)
        la, lb = pltpu.roll(a, 7, 0), pltpu.roll(b, 7, 0)
        before = (jnp.where(first, rb, ra), jnp.where(first, ra, rb))
        after = (jnp.where(last, lb, la), jnp.where(last, la, lb))
        for h in range(2):
            v = core[c][h]
            xm, xp = pltpu.roll(v, 1, 1), pltpu.roll(v, 127, 1)
            zm, zp = src[c, tile + h - 2], src[c, tile + h + 2]
            near = (xp + xm) + (after[h] + before[h]) + (zp + zm)
            advect = wind[0][h] * (xp - xm) + wind[1][h] * (after[h] - before[h]) + wind[2][h] * (zp - zm)
            out = (new * KEEP) * v + ((new * NEAR) * near - advect)
            if kind:
                out = out + old * base[c, tile + h]
            put(c, h, out)


def kernel(states, rate_in, out, rate, w0, w1, w2, w3, w4, w5, jump, got, total, tots, path,
           load_sem, halo_send, halo_recv, up_send, up_recv, row_send, row_recv, down_send, down_recv, own_sem):
    tm, gz = lax.axis_index("tm"), lax.axis_index("gz")
    zi, row = lax.rem(tm, RING), lax.div(tm, RING)
    above, below = lax.rem(gz + 1, SLABS), lax.rem(gz + SLABS - 1, SLABS)
    far = lax.rem(gz, 2)
    start = row * RING

    load = pltpu.make_async_copy(states, w0.at[:, pl.ds(2 * WIDE, 2 * OWN)], load_sem.at[0])
    load.start()
    load_rate = pltpu.make_async_copy(rate_in, rate, load_sem.at[1])
    load_rate.start()
    barrier = pltpu.get_barrier_semaphore()
    for peer in (above, below):
        pl.semaphore_signal(barrier, inc=1, device_id={"gz": peer}, device_id_type=MESH)
    for q in range(1, RING):
        pl.semaphore_signal(barrier, inc=1, device_id={"tm": start + lax.rem(zi + q, RING)}, device_id_type=MESH)

    def greet(q, carry):
        pl.semaphore_signal(barrier, inc=1, device_id={"tm": q * RING + zi}, device_id_type=MESH)
        return carry

    lax.fori_loop(0, row, greet, 0)
    pl.semaphore_wait(barrier, 2 + (RING - 1) + (ROWS - 1 - row))

    down_halo = pltpu.make_async_remote_copy(
        states.at[:, pl.ds(0, 2 * WIDE)], w0.at[:, pl.ds(2 * (OWN + WIDE), 2 * WIDE)], halo_send.at[0], halo_recv.at[1],
        device_id={"gz": below}, device_id_type=MESH)
    up_halo = pltpu.make_async_remote_copy(
        states.at[:, pl.ds(2 * (OWN - WIDE), 2 * WIDE)], w0.at[:, pl.ds(0, 2 * WIDE)], halo_send.at[1], halo_recv.at[0],
        device_id={"gz": above}, device_id_type=MESH)
    down_halo.start()
    up_halo.start()

    @pl.when(tm == 0)
    def _():
        pltpu.make_async_copy(states, out, own_sem.at[0]).start()

    works = (w0, w1, w2, w3, w4, w5)
    keep_own = jnp.where(tm == 0, 0.0, 1.0)

    def stages(first_plane, count, at_once):
        for k in range(1, 2 * 3 + 1):
            src, base = works[k - 1], works[3 * ((k - 1) // 3)]
            kind = (k - 1) % 3
            begin = first_plane(k)

            def one_plane(plane, k, src, base, kind):
                if k < 6:
                    def put(c, h, value):
                        works[k][c, 2 * plane + h] = value
                else:
                    damp = [jnp.exp(rate[2 * (plane - WIDE) + h] * (-1.0 / SLICES)) * keep_own for h in range(2)]

                    def put(c, h, value):
                        jump[c, 2 * (plane - WIDE) + h] = value - damp[h] * w0[c, 2 * plane + h]

                stage_plane(kind, src, base, plane, put)

            def turn(i, carry, k=k, src=src, base=base, kind=kind, begin=begin):
                for j in range(at_once[k - 1]):
                    one_plane(begin + at_once[k - 1] * i + j, k, src, base, kind)
                return carry

            turns = count(k) // at_once[k - 1]
            if turns == 1:
                turn(0, 0)
            else:
                lax.fori_loop(0, turns, turn, 0)

    bases = (6, 10 - 8 * far, 2 + 8 * far)

    def tile_of(group, k):
        if group < 3:
            return 2 * bases[group] + k
        return k + jnp.where(k >= 4, 24, 0)

    def send_up(group):
        for q in (4, 3, 5, 2, 6, 1, 7):
            peer = lax.rem(zi + q, RING)
            pltpu.make_async_remote_copy(
                jump.at[:, tile_of(group, peer)], got.at[group, zi], up_send.at[group], up_recv.at[group],
                device_id={"tm": start + peer}, device_id_type=MESH).start()

    def all_of(buf, send, recv):
        return pltpu.make_async_remote_copy(
            buf.at[pl.ds(0, RING - 1)], buf.at[pl.ds(0, RING - 1)], send, recv,
            device_id={"tm": tm}, device_id_type=MESH)

    def damp_of(group):
        return jnp.exp(rate[tile_of(group, zi)] * (-1.0 / SLICES))

    def sum_row(group):
        all_of(got.at[group], up_send.at[group], up_recv.at[group]).wait_recv()
        mine = tile_of(group, zi)
        for c in range(3):
            got[group, zi, c] = jump[c, mine]
        damp = damp_of(group)
        acc = [got[group, 0, c] for c in range(3)]
        for z in range(1, RING):
            acc = [damp * acc[c] + got[group, z, c] for c in range(3)]
        for c in range(3):
            total[group, c] = acc[c]

        def tell(later, carry):
            pltpu.make_async_remote_copy(
                total.at[group], tots.at[group, row], row_send.at[group, later], row_recv.at[group, row],
                device_id={"tm": later * RING + zi}, device_id_type=MESH).start()
            return carry

        lax.fori_loop(row + 1, ROWS, tell, 0)

    def send_down(group):
        damp = damp_of(group)
        eighth = damp * damp
        eighth = eighth * eighth
        eighth = eighth * eighth

        def add(q, carry):
            pltpu.make_async_remote_copy(
                total.at[group], tots.at[group, q], row_send.at[group, q], row_recv.at[group, q],
                device_id={"tm": q * RING + zi}, device_id_type=MESH).wait_recv()
            return tuple(eighth * carry[c] + tots[group, q, c] for c in range(3))

        acc = lax.fori_loop(0, row, add, tuple(jnp.zeros((8, 128), jnp.float32) for _ in range(3)))
        for z in range(RING):
            for c in range(3):
                path[group, z, c] = acc[c]
            if z < RING - 1:
                acc = [damp * acc[c] + got[group, z, c] for c in range(3)]
        mine = tile_of(group, zi)
        for q in (4, 3, 5, 2, 6, 1, 7):
            peer = lax.rem(zi + q, RING)

            @pl.when(start + peer > 0)
            def _():
                pltpu.make_async_remote_copy(
                    path.at[group, peer], out.at[:, mine], down_send.at[group, q], down_recv.at[group, q],
                    device_id={"tm": start + peer}, device_id_type=MESH).start()

        @pl.when(tm > 0)
        def _():
            pltpu.make_async_copy(path.at[group, zi], out.at[:, mine], own_sem.at[group]).start()

    load.wait()
    load_rate.wait()
    stages(lambda k: WIDE + k, lambda k: OWN - 2 * k, (7, 6, 5, 8, 6, 4))
    send_up(0)

    def side(upper):
        @pl.when(upper == 0)
        def _():
            up_halo.wait_recv()

        @pl.when(upper == 1)
        def _():
            down_halo.wait_recv()

        stages(lambda k: jnp.where(upper == 1, OWN + WIDE - k, k), lambda k: WIDE, (6,) * 6)

    side(1 - far)
    send_up(1)
    side(far)
    send_up(2)
    send_up(3)
    sum_row(0)
    sum_row(1)
    send_down(0)
    sum_row(2)
    send_down(1)
    sum_row(3)
    send_down(2)
    send_down(3)

    for group in range(GROUPS):
        mine = tile_of(group, zi)
        all_of(got.at[group], up_send.at[group], up_recv.at[group]).wait_send()

        def told(later, carry, group=group):
            pltpu.make_async_remote_copy(
                total.at[group], tots.at[group, row], row_send.at[group, later], row_recv.at[group, row],
                device_id={"tm": later * RING + zi}, device_id_type=MESH).wait_send()
            return carry

        lax.fori_loop(row + 1, ROWS, told, 0)
        for q in range(1, RING):
            peer, source = lax.rem(zi + q, RING), lax.rem(zi + RING - q, RING)

            @pl.when(start + peer > 0)
            def _():
                pltpu.make_async_remote_copy(
                    path.at[group, peer], out.at[:, mine], down_send.at[group, q], down_recv.at[group, q],
                    device_id={"tm": start + peer}, device_id_type=MESH).wait_send()

            @pl.when(tm > 0)
            def _():
                pltpu.make_async_remote_copy(
                    path.at[group, zi], out.at[:, tile_of(group, source)], down_send.at[group, q], down_recv.at[group, q],
                    device_id={"tm": start + source}, device_id_type=MESH).wait_recv()

        @pl.when(tm > 0)
        def _():
            pltpu.make_async_copy(path.at[group, zi], out.at[:, mine], own_sem.at[group]).wait()

    @pl.when(tm == 0)
    def _():
        pltpu.make_async_copy(states, out, own_sem.at[0]).wait()

    down_halo.wait_send()
    up_halo.wait_send()


def shards(states, rate):
    f32 = jnp.float32
    work = pltpu.VMEM((3, 2 * SPAN, 8, 128), f32)
    dma = pltpu.SemaphoreType.DMA
    out = pl.pallas_call(
        kernel,
        out_shape=jax.ShapeDtypeStruct((3, 2 * OWN, 8, 128), f32),
        in_specs=[pl.BlockSpec(memory_space=pltpu.HBM), pl.BlockSpec(memory_space=pltpu.HBM)],
        out_specs=pl.BlockSpec(memory_space=pl.ANY),
        scratch_shapes=[pltpu.VMEM((2 * OWN, 8, 128), f32)] + [work] * 6 + [
            pltpu.VMEM((3, 2 * OWN, 8, 128), f32),
            pltpu.VMEM((GROUPS, RING, 3, 8, 128), f32),
            pltpu.VMEM((GROUPS, 3, 8, 128), f32),
            pltpu.VMEM((GROUPS, ROWS, 3, 8, 128), f32),
            pltpu.VMEM((GROUPS, RING, 3, 8, 128), f32),
            dma((2,)), dma((2,)), dma((2,)), dma((GROUPS,)), dma((GROUPS,)),
            dma((GROUPS, ROWS)), dma((GROUPS, ROWS)), dma((GROUPS, RING)), dma((GROUPS, RING)), dma((GROUPS,)),
        ],
        compiler_params=pltpu.CompilerParams(collective_id=0, has_side_effects=True, vmem_limit_bytes=32 * 1024 * 1024),
    )(pltpu.with_memory_space_constraint(states.reshape(3, 2 * OWN, 8, 128), pltpu.HBM), pltpu.with_memory_space_constraint(rate.reshape(2 * OWN, 8, 128), pltpu.HBM))
    return out.reshape(1, 3, OWN, 16, 128)


def solution(mesh):
    return jax.shard_map(
        shards,
        mesh=mesh,
        in_specs=(P("tm", None, "gz", None, None), P("gz", None, None)),
        out_specs=P("tm", None, "gz", None, None),
        check_vma=False,
    )
```

```python
import jax
import jax.numpy as jnp
from jax import lax
from jax.experimental import pallas as pl
from jax.experimental.pallas import tpu as pltpu
from jax.sharding import PartitionSpec as P

STEPS = 2
VISCOSITY = 0.05
TIME_STEP = 0.2
SLICES = 64
RING = 8
ROWS = 8
SLABS = 4
WIDE = 3 * STEPS
NEXT = 4
OWN = 16
SPAN = OWN + 2 * WIDE
GROUPS = 4
MESH = pl.DeviceIdType.MESH

KEEP = 1.0 - 6.0 * VISCOSITY * TIME_STEP
NEAR = VISCOSITY * TIME_STEP
HALF = 0.5 * TIME_STEP
WEIGHTS = ((0.0, 1.0), (0.75, 0.25), (1.0 / 3.0, 2.0 / 3.0))


def stage_plane(kind, src, base, plane, put):
    old, new = WEIGHTS[kind]
    row = lax.broadcasted_iota(jnp.int32, (8, 128), 0)
    first, last = row == 0, row == 7
    tile = 2 * plane
    core = [[src[c, tile + h] for h in range(2)] for c in range(3)]
    wind = [[core[c][h] * (new * HALF) for h in range(2)] for c in range(3)]
    for c in range(3):
        a, b = core[c]
        ra, rb = pltpu.roll(a, 1, 0), pltpu.roll(b, 1, 0)
        la, lb = pltpu.roll(a, 7, 0), pltpu.roll(b, 7, 0)
        before = (jnp.where(first, rb, ra), jnp.where(first, ra, rb))
        after = (jnp.where(last, lb, la), jnp.where(last, la, lb))
        for h in range(2):
            v = core[c][h]
            xm, xp = pltpu.roll(v, 1, 1), pltpu.roll(v, 127, 1)
            zm, zp = src[c, tile + h - 2], src[c, tile + h + 2]
            near = (xp + xm) + (after[h] + before[h]) + (zp + zm)
            advect = wind[0][h] * (xp - xm) + wind[1][h] * (after[h] - before[h]) + wind[2][h] * (zp - zm)
            out = (new * KEEP) * v + ((new * NEAR) * near - advect)
            if kind:
                out = out + old * base[c, tile + h]
            put(c, h, out)


def kernel(states, rate_in, out, rate, w0, w1, w2, w3, w4, w5, jump, got, total, tots, path,
           load_sem, halo_send, halo_recv, up_send, up_recv, row_send, row_recv, down_send, down_recv, own_sem):
    tm, gz = lax.axis_index("tm"), lax.axis_index("gz")
    zi, row = tm & (RING - 1), tm // RING
    above, below = (gz + 1) & (SLABS - 1), (gz + SLABS - 1) & (SLABS - 1)
    far = gz & 1
    start = row * RING

    load = pltpu.make_async_copy(states, w0.at[:, pl.ds(2 * WIDE, 2 * OWN)], load_sem.at[0])
    load.start()
    load_rate = pltpu.make_async_copy(rate_in, rate, load_sem.at[1])
    load_rate.start()
    barrier = pltpu.get_barrier_semaphore()
    for peer in (above, below):
        pl.semaphore_signal(barrier, inc=1, device_id={"gz": peer}, device_id_type=MESH)
    for q in range(1, RING):
        pl.semaphore_signal(barrier, inc=1, device_id={"tm": start + ((zi + q) & (RING - 1))}, device_id_type=MESH)

    def greet(q, carry):
        pl.semaphore_signal(barrier, inc=1, device_id={"tm": q * RING + zi}, device_id_type=MESH)
        return carry

    lax.fori_loop(0, row, greet, 0)
    def halo(upper, outer):
        planes = WIDE - NEXT if outer else NEXT
        if upper:
            source, target = (NEXT if outer else 0), OWN + WIDE + (NEXT if outer else 0)
        else:
            source, target = OWN - (WIDE if outer else NEXT), (0 if outer else WIDE - NEXT)
        return pltpu.make_async_remote_copy(
            w0.at[:, pl.ds(2 * (WIDE + source), 2 * planes)], w0.at[:, pl.ds(2 * target, 2 * planes)],
            halo_send.at[upper, outer], halo_recv.at[upper, outer],
            device_id={"gz": below if upper else above}, device_id_type=MESH)

    @pl.when(tm == 0)
    def _():
        pltpu.make_async_copy(states, out, own_sem.at[0]).start()

    works = (w0, w1, w2, w3, w4, w5)
    keep_own = jnp.where(tm == 0, 0.0, 1.0)

    def stages(first_plane, count, at_once, ks=range(1, 7)):
        for k in ks:
            src, base = works[k - 1], works[3 * ((k - 1) // 3)]
            kind = (k - 1) % 3
            begin = first_plane(k)

            def one_plane(plane, k, src, base, kind):
                if k < 6:
                    def put(c, h, value):
                        works[k][c, 2 * plane + h] = value
                else:
                    damp = [jnp.exp(rate[2 * (plane - WIDE) + h] * (-1.0 / SLICES)) * keep_own for h in range(2)]

                    def put(c, h, value):
                        jump[c, 2 * (plane - WIDE) + h] = value - damp[h] * w0[c, 2 * plane + h]

                stage_plane(kind, src, base, plane, put)

            def turn(i, carry, k=k, src=src, base=base, kind=kind, begin=begin):
                for j in range(at_once[k - 1]):
                    one_plane(begin + at_once[k - 1] * i + j, k, src, base, kind)
                return carry

            turns = count(k) // at_once[k - 1]
            if turns == 1:
                turn(0, 0)
            else:
                lax.fori_loop(0, turns, turn, 0)

    bases = (6, 10 - 8 * far, 2 + 8 * far)

    def tile_of(group, k):
        if group < 3:
            return 2 * bases[group] + k
        return k + jnp.where(k >= 4, 24, 0)

    def send_up(group):
        for q in (4, 3, 5, 2, 6, 1, 7):
            peer = ((zi + q) & (RING - 1))
            pltpu.make_async_remote_copy(
                jump.at[:, tile_of(group, peer)], got.at[group, zi], up_send.at[group], up_recv.at[group],
                device_id={"tm": start + peer}, device_id_type=MESH).start()

    def all_of(buf, send, recv):
        return pltpu.make_async_remote_copy(
            buf.at[pl.ds(0, RING - 1)], buf.at[pl.ds(0, RING - 1)], send, recv,
            device_id={"tm": tm}, device_id_type=MESH)

    def damp_of(group):
        return jnp.exp(rate[tile_of(group, zi)] * (-1.0 / SLICES))

    def sum_row(group):
        all_of(got.at[group], up_send.at[group], up_recv.at[group]).wait_recv()
        mine = tile_of(group, zi)
        for c in range(3):
            got[group, zi, c] = jump[c, mine]
        damp = damp_of(group)
        acc = [got[group, 0, c] for c in range(3)]
        for z in range(1, RING):
            acc = [damp * acc[c] + got[group, z, c] for c in range(3)]
        for c in range(3):
            total[group, c] = acc[c]

        def tell(later, carry):
            pltpu.make_async_remote_copy(
                total.at[group], tots.at[group, row], row_send.at[group, later], row_recv.at[group, row],
                device_id={"tm": later * RING + zi}, device_id_type=MESH).start()
            return carry

        lax.fori_loop(row + 1, ROWS, tell, 0)

    def send_down(group):
        damp = damp_of(group)
        eighth = damp * damp
        eighth = eighth * eighth
        eighth = eighth * eighth

        def add(q, carry):
            pltpu.make_async_remote_copy(
                total.at[group], tots.at[group, q], row_send.at[group, q], row_recv.at[group, q],
                device_id={"tm": q * RING + zi}, device_id_type=MESH).wait_recv()
            return tuple(eighth * carry[c] + tots[group, q, c] for c in range(3))

        acc = lax.fori_loop(0, row, add, tuple(jnp.zeros((8, 128), jnp.float32) for _ in range(3)))
        for z in range(RING):
            for c in range(3):
                path[group, z, c] = acc[c]
            if z < RING - 1:
                acc = [damp * acc[c] + got[group, z, c] for c in range(3)]
        mine = tile_of(group, zi)
        for q in (4, 3, 5, 2, 6, 1, 7):
            peer = ((zi + q) & (RING - 1))

            @pl.when(start + peer > 0)
            def _():
                pltpu.make_async_remote_copy(
                    path.at[group, peer], out.at[:, mine], down_send.at[group, q], down_recv.at[group, q],
                    device_id={"tm": start + peer}, device_id_type=MESH).start()

        @pl.when(tm > 0)
        def _():
            pltpu.make_async_copy(path.at[group, zi], out.at[:, mine], own_sem.at[group]).start()

    load.wait()
    load_rate.wait()
    inside = lambda ks: stages(lambda k: WIDE + k, lambda k: OWN - 2 * k, (7, 6, 5, 8, 6, 4), ks)
    inside(range(1, 5))
    pl.semaphore_wait(barrier, 2 + (RING - 1) + (ROWS - 1 - row))


    for upper in (0, 1):
        @pl.when(upper == 1 - far)
        def _(upper=upper):
            halo(1 - upper, 0).start()
            halo(upper, 0).start()
            halo(upper, 1).start()
            halo(1 - upper, 1).start()

    inside(range(5, 7))
    send_up(0)

    def halo_wait(upper, outers):
        for choice in (0, 1):
            @pl.when(upper == choice)
            def _(choice=choice):
                for outer in outers:
                    halo(choice, outer).wait_recv()

    def side(upper, skip, planes):
        stages(lambda k: jnp.where(upper == 1, SPAN - WIDE + skip - k, WIDE - skip - planes + k), lambda k: planes, (planes,) * 6)

    near_upper, far_upper = 1 - far, far
    halo_wait(near_upper, (0, 1))
    side(near_upper, 0, WIDE)
    send_up(1)
    halo_wait(far_upper, (0,))
    side(far_upper, 0, NEXT)
    send_up(2)
    halo_wait(far_upper, (1,))
    side(far_upper, NEXT, WIDE - NEXT)
    send_up(3)
    sum_row(0)
    sum_row(1)
    send_down(0)
    sum_row(2)
    send_down(1)
    sum_row(3)
    send_down(2)
    send_down(3)

    for group in range(GROUPS):
        mine = tile_of(group, zi)
        all_of(got.at[group], up_send.at[group], up_recv.at[group]).wait_send()

        def told(later, carry, group=group):
            pltpu.make_async_remote_copy(
                total.at[group], tots.at[group, row], row_send.at[group, later], row_recv.at[group, row],
                device_id={"tm": later * RING + zi}, device_id_type=MESH).wait_send()
            return carry

        lax.fori_loop(row + 1, ROWS, told, 0)
        for q in range(1, RING):
            peer, source = ((zi + q) & (RING - 1)), ((zi + RING - q) & (RING - 1))

            @pl.when(start + peer > 0)
            def _():
                pltpu.make_async_remote_copy(
                    path.at[group, peer], out.at[:, mine], down_send.at[group, q], down_recv.at[group, q],
                    device_id={"tm": start + peer}, device_id_type=MESH).wait_send()

            @pl.when(tm > 0)
            def _():
                pltpu.make_async_remote_copy(
                    path.at[group, zi], out.at[:, tile_of(group, source)], down_send.at[group, q], down_recv.at[group, q],
                    device_id={"tm": start + source}, device_id_type=MESH).wait_recv()

        @pl.when(tm > 0)
        def _():
            pltpu.make_async_copy(path.at[group, zi], out.at[:, mine], own_sem.at[group]).wait()

    @pl.when(tm == 0)
    def _():
        pltpu.make_async_copy(states, out, own_sem.at[0]).wait()

    for upper in (0, 1):
        for outer in (0, 1):
            halo(upper, outer).wait_send()


def shards(states, rate):
    f32 = jnp.float32
    work = pltpu.VMEM((3, 2 * SPAN, 8, 128), f32)
    dma = pltpu.SemaphoreType.DMA
    out = pl.pallas_call(
        kernel,
        out_shape=jax.ShapeDtypeStruct((3, 2 * OWN, 8, 128), f32),
        in_specs=[pl.BlockSpec(memory_space=pltpu.HBM), pl.BlockSpec(memory_space=pltpu.HBM)],
        out_specs=pl.BlockSpec(memory_space=pl.ANY),
        scratch_shapes=[pltpu.VMEM((2 * OWN, 8, 128), f32)] + [work] * 6 + [
            pltpu.VMEM((3, 2 * OWN, 8, 128), f32),
            pltpu.VMEM((GROUPS, RING, 3, 8, 128), f32),
            pltpu.VMEM((GROUPS, 3, 8, 128), f32),
            pltpu.VMEM((GROUPS, ROWS, 3, 8, 128), f32),
            pltpu.VMEM((GROUPS, RING, 3, 8, 128), f32),
            dma((2,)), dma((2, 2)), dma((2, 2)), dma((GROUPS,)), dma((GROUPS,)),
            dma((GROUPS, ROWS)), dma((GROUPS, ROWS)), dma((GROUPS, RING)), dma((GROUPS, RING)), dma((GROUPS,)),
        ],
        compiler_params=pltpu.CompilerParams(collective_id=0, has_side_effects=True, vmem_limit_bytes=32 * 1024 * 1024),
    )(pltpu.with_memory_space_constraint(states.reshape(3, 2 * OWN, 8, 128), pltpu.HBM), pltpu.with_memory_space_constraint(rate.reshape(2 * OWN, 8, 128), pltpu.HBM))
    return out.reshape(1, 3, OWN, 16, 128)


def solution(mesh):
    return jax.shard_map(
        shards,
        mesh=mesh,
        in_specs=(P("tm", None, "gz", None, None), P("gz", None, None)),
        out_specs=P("tm", None, "gz", None, None),
        check_vma=False,
    )
```

```python
import jax
import jax.numpy as jnp
from jax import lax
from jax.experimental import pallas as pl
from jax.experimental.pallas import tpu as pltpu
from jax.sharding import PartitionSpec as P

STEPS = 2
VISCOSITY = 0.05
TIME_STEP = 0.2
SLICES = 64
RING = 8
ROWS = 8
SLABS = 4
WIDE = 3 * STEPS
NEXT = 4
OWN = 16
SPAN = OWN + 2 * WIDE
GROUPS = 4
MESH = pl.DeviceIdType.MESH

KEEP = 1.0 - 6.0 * VISCOSITY * TIME_STEP
NEAR = VISCOSITY * TIME_STEP
HALF = 0.5 * TIME_STEP
WEIGHTS = ((0.0, 1.0), (0.75, 0.25), (1.0 / 3.0, 2.0 / 3.0))


def stage_plane(kind, src, base, plane, put):
    old, new = WEIGHTS[kind]
    row = lax.broadcasted_iota(jnp.int32, (8, 128), 0)
    first, last = row == 0, row == 7
    tile = 2 * plane
    core = [[src[c, tile + h] for h in range(2)] for c in range(3)]
    wind = [[core[c][h] * (new * HALF) for h in range(2)] for c in range(3)]
    for c in range(3):
        a, b = core[c]
        ra, rb = pltpu.roll(a, 1, 0), pltpu.roll(b, 1, 0)
        la, lb = pltpu.roll(a, 7, 0), pltpu.roll(b, 7, 0)
        before = (jnp.where(first, rb, ra), jnp.where(first, ra, rb))
        after = (jnp.where(last, lb, la), jnp.where(last, la, lb))
        for h in range(2):
            v = core[c][h]
            xm, xp = pltpu.roll(v, 1, 1), pltpu.roll(v, 127, 1)
            zm, zp = src[c, tile + h - 2], src[c, tile + h + 2]
            near = (xp + xm) + (after[h] + before[h]) + (zp + zm)
            advect = wind[0][h] * (xp - xm) + wind[1][h] * (after[h] - before[h]) + wind[2][h] * (zp - zm)
            out = (new * KEEP) * v + ((new * NEAR) * near - advect)
            if kind:
                out = out + old * base[c, tile + h]
            put(c, h, out)


def kernel(states, rate_in, out, rate, w0, w1, w2, w3, w4, w5, jump, got, total, tots, path,
           load_sem, halo_send, halo_recv, up_send, up_recv, row_send, row_recv, down_send, down_recv, own_sem):
    tm, gz = lax.axis_index("tm"), lax.axis_index("gz")
    zi, row = tm & (RING - 1), tm // RING
    above, below = (gz + 1) & (SLABS - 1), (gz + SLABS - 1) & (SLABS - 1)
    far = gz & 1
    start = row * RING

    load = pltpu.make_async_copy(states, w0.at[:, pl.ds(2 * WIDE, 2 * OWN)], load_sem.at[0])
    load.start()
    load_rate = pltpu.make_async_copy(rate_in, rate, load_sem.at[1])
    load_rate.start()
    barrier = pltpu.get_barrier_semaphore()
    for peer in (above, below):
        pl.semaphore_signal(barrier, inc=1, device_id={"gz": peer}, device_id_type=MESH)
    for q in range(1, RING):
        pl.semaphore_signal(barrier, inc=1, device_id={"tm": start + ((zi + q) & (RING - 1))}, device_id_type=MESH)

    def greet(q, carry):
        pl.semaphore_signal(barrier, inc=1, device_id={"tm": q * RING + zi}, device_id_type=MESH)
        return carry

    lax.fori_loop(0, row, greet, 0)
    def halo(upper, outer):
        planes = WIDE - NEXT if outer else NEXT
        if upper:
            source, target = (NEXT if outer else 0), OWN + WIDE + (NEXT if outer else 0)
        else:
            source, target = OWN - (WIDE if outer else NEXT), (0 if outer else WIDE - NEXT)
        return pltpu.make_async_remote_copy(
            w0.at[:, pl.ds(2 * (WIDE + source), 2 * planes)], w0.at[:, pl.ds(2 * target, 2 * planes)],
            halo_send.at[upper, outer], halo_recv.at[upper, outer],
            device_id={"gz": below if upper else above}, device_id_type=MESH)

    @pl.when(tm == 0)
    def _():
        pltpu.make_async_copy(states, out, own_sem.at[0]).start()

    works = (w0, w1, w2, w3, w4, w5)
    keep_own = jnp.where(tm == 0, 0.0, 1.0)

    def stages(first_plane, count, at_once, ks=range(1, 7)):
        for k in ks:
            src, base = works[k - 1], works[3 * ((k - 1) // 3)]
            kind = (k - 1) % 3
            begin = first_plane(k)

            def one_plane(plane, k, src, base, kind):
                if k < 6:
                    def put(c, h, value):
                        works[k][c, 2 * plane + h] = value
                else:
                    damp = [jnp.exp(rate[2 * (plane - WIDE) + h] * (-1.0 / SLICES)) * keep_own for h in range(2)]

                    def put(c, h, value):
                        jump[c, 2 * (plane - WIDE) + h] = value - damp[h] * w0[c, 2 * plane + h]

                stage_plane(kind, src, base, plane, put)

            def turn(i, carry, k=k, src=src, base=base, kind=kind, begin=begin):
                for j in range(at_once[k - 1]):
                    one_plane(begin + at_once[k - 1] * i + j, k, src, base, kind)
                return carry

            turns = count(k) // at_once[k - 1]
            if turns == 1:
                turn(0, 0)
            else:
                lax.fori_loop(0, turns, turn, 0)

    bases = (6, 10 - 8 * far, 2 + 8 * far)

    def tile_of(group, k):
        if group < 3:
            return 2 * bases[group] + k
        return k + jnp.where(k >= 4, 24, 0)

    def send_up(group):
        for q in (4, 3, 5, 2, 6, 1, 7):
            peer = ((zi + q) & (RING - 1))
            pltpu.make_async_remote_copy(
                jump.at[:, tile_of(group, peer)], got.at[group, zi], up_send.at[group], up_recv.at[group],
                device_id={"tm": start + peer}, device_id_type=MESH).start()

    def all_of(buf, send, recv):
        return pltpu.make_async_remote_copy(
            buf.at[pl.ds(0, RING - 1)], buf.at[pl.ds(0, RING - 1)], send, recv,
            device_id={"tm": tm}, device_id_type=MESH)

    def damp_of(group):
        return jnp.exp(rate[tile_of(group, zi)] * (-1.0 / SLICES))

    def sum_row(group):
        all_of(got.at[group], up_send.at[group], up_recv.at[group]).wait_recv()
        mine = tile_of(group, zi)
        for c in range(3):
            got[group, zi, c] = jump[c, mine]
        damp = damp_of(group)
        acc = [got[group, 0, c] for c in range(3)]
        for z in range(1, RING):
            acc = [damp * acc[c] + got[group, z, c] for c in range(3)]
        for c in range(3):
            total[group, c] = acc[c]

        def tell(later, carry):
            pltpu.make_async_remote_copy(
                total.at[group], tots.at[group, row], row_send.at[group, later], row_recv.at[group, row],
                device_id={"tm": later * RING + zi}, device_id_type=MESH).start()
            return carry

        lax.fori_loop(0, ROWS - 1 - row, lambda i, carry: tell(ROWS - 1 - i, carry), 0)

    def send_down(group):
        damp = damp_of(group)
        eighth = damp * damp
        eighth = eighth * eighth
        eighth = eighth * eighth

        def add(q, carry):
            pltpu.make_async_remote_copy(
                total.at[group], tots.at[group, q], row_send.at[group, q], row_recv.at[group, q],
                device_id={"tm": q * RING + zi}, device_id_type=MESH).wait_recv()
            return tuple(eighth * carry[c] + tots[group, q, c] for c in range(3))

        acc = lax.fori_loop(0, row, add, tuple(jnp.zeros((8, 128), jnp.float32) for _ in range(3)))
        for z in range(RING):
            for c in range(3):
                path[group, z, c] = acc[c]
            if z < RING - 1:
                acc = [damp * acc[c] + got[group, z, c] for c in range(3)]
        mine = tile_of(group, zi)
        for q in (4, 3, 5, 2, 6, 1, 7):
            peer = ((zi + q) & (RING - 1))

            @pl.when(start + peer > 0)
            def _():
                pltpu.make_async_remote_copy(
                    path.at[group, peer], out.at[:, mine], down_send.at[group, q], down_recv.at[group, q],
                    device_id={"tm": start + peer}, device_id_type=MESH).start()

        @pl.when(tm > 0)
        def _():
            pltpu.make_async_copy(path.at[group, zi], out.at[:, mine], own_sem.at[group]).start()

    load.wait()
    load_rate.wait()
    inside = lambda ks: stages(lambda k: WIDE + k, lambda k: OWN - 2 * k, (7, 6, 5, 8, 6, 4), ks)
    inside(range(1, 5))
    pl.semaphore_wait(barrier, 2 + (RING - 1) + (ROWS - 1 - row))


    for upper in (0, 1):
        @pl.when(upper == 1 - far)
        def _(upper=upper):
            halo(1 - upper, 0).start()
            halo(upper, 0).start()
            halo(upper, 1).start()
            halo(1 - upper, 1).start()

    inside(range(5, 7))
    send_up(0)

    def halo_wait(upper, outers):
        for choice in (0, 1):
            @pl.when(upper == choice)
            def _(choice=choice):
                for outer in outers:
                    halo(choice, outer).wait_recv()

    def side(upper, skip, planes):
        stages(lambda k: jnp.where(upper == 1, SPAN - WIDE + skip - k, WIDE - skip - planes + k), lambda k: planes, (planes,) * 6)

    near_upper, far_upper = 1 - far, far
    halo_wait(near_upper, (0, 1))
    side(near_upper, 0, WIDE)
    send_up(1)
    halo_wait(far_upper, (0,))
    side(far_upper, 0, NEXT)
    send_up(2)
    sum_row(0)
    halo_wait(far_upper, (1,))
    side(far_upper, NEXT, WIDE - NEXT)
    send_up(3)
    sum_row(1)
    send_down(0)
    sum_row(2)
    send_down(1)
    sum_row(3)
    send_down(2)
    send_down(3)

    for group in range(GROUPS):
        mine = tile_of(group, zi)
        all_of(got.at[group], up_send.at[group], up_recv.at[group]).wait_send()

        def told(later, carry, group=group):
            pltpu.make_async_remote_copy(
                total.at[group], tots.at[group, row], row_send.at[group, later], row_recv.at[group, row],
                device_id={"tm": later * RING + zi}, device_id_type=MESH).wait_send()
            return carry

        lax.fori_loop(row + 1, ROWS, told, 0)
        for q in range(1, RING):
            peer, source = ((zi + q) & (RING - 1)), ((zi + RING - q) & (RING - 1))

            @pl.when(start + peer > 0)
            def _():
                pltpu.make_async_remote_copy(
                    path.at[group, peer], out.at[:, mine], down_send.at[group, q], down_recv.at[group, q],
                    device_id={"tm": start + peer}, device_id_type=MESH).wait_send()

            @pl.when(tm > 0)
            def _():
                pltpu.make_async_remote_copy(
                    path.at[group, zi], out.at[:, tile_of(group, source)], down_send.at[group, q], down_recv.at[group, q],
                    device_id={"tm": start + source}, device_id_type=MESH).wait_recv()

        @pl.when(tm > 0)
        def _():
            pltpu.make_async_copy(path.at[group, zi], out.at[:, mine], own_sem.at[group]).wait()

    @pl.when(tm == 0)
    def _():
        pltpu.make_async_copy(states, out, own_sem.at[0]).wait()

    for upper in (0, 1):
        for outer in (0, 1):
            halo(upper, outer).wait_send()


def shards(states, rate):
    f32 = jnp.float32
    work = pltpu.VMEM((3, 2 * SPAN, 8, 128), f32)
    dma = pltpu.SemaphoreType.DMA
    out = pl.pallas_call(
        kernel,
        out_shape=jax.ShapeDtypeStruct((3, 2 * OWN, 8, 128), f32),
        in_specs=[pl.BlockSpec(memory_space=pltpu.HBM), pl.BlockSpec(memory_space=pltpu.HBM)],
        out_specs=pl.BlockSpec(memory_space=pl.ANY),
        scratch_shapes=[pltpu.VMEM((2 * OWN, 8, 128), f32)] + [work] * 6 + [
            pltpu.VMEM((3, 2 * OWN, 8, 128), f32),
            pltpu.VMEM((GROUPS, RING, 3, 8, 128), f32),
            pltpu.VMEM((GROUPS, 3, 8, 128), f32),
            pltpu.VMEM((GROUPS, ROWS, 3, 8, 128), f32),
            pltpu.VMEM((GROUPS, RING, 3, 8, 128), f32),
            dma((2,)), dma((2, 2)), dma((2, 2)), dma((GROUPS,)), dma((GROUPS,)),
            dma((GROUPS, ROWS)), dma((GROUPS, ROWS)), dma((GROUPS, RING)), dma((GROUPS, RING)), dma((GROUPS,)),
        ],
        compiler_params=pltpu.CompilerParams(collective_id=0, has_side_effects=True, vmem_limit_bytes=32 * 1024 * 1024),
    )(pltpu.with_memory_space_constraint(states.reshape(3, 2 * OWN, 8, 128), pltpu.HBM), pltpu.with_memory_space_constraint(rate.reshape(2 * OWN, 8, 128), pltpu.HBM))
    return out.reshape(1, 3, OWN, 16, 128)


def solution(mesh):
    return jax.shard_map(
        shards,
        mesh=mesh,
        in_specs=(P("tm", None, "gz", None, None), P("gz", None, None)),
        out_specs=P("tm", None, "gz", None, None),
        check_vma=False,
    )
```

```python
import jax
import jax.numpy as jnp
from jax import lax
from jax.experimental import pallas as pl
from jax.experimental.pallas import tpu as pltpu
from jax.sharding import PartitionSpec as P

STEPS = 2
VISCOSITY = 0.05
TIME_STEP = 0.2
SLICES = 64
RING = 8
ROWS = 8
SLABS = 4
WIDE = 3 * STEPS
NEXT = 2
OWN = 16
SPAN = OWN + 2 * WIDE
GROUPS = 4
MESH = pl.DeviceIdType.MESH

KEEP = 1.0 - 6.0 * VISCOSITY * TIME_STEP
NEAR = VISCOSITY * TIME_STEP
HALF = 0.5 * TIME_STEP
WEIGHTS = ((0.0, 1.0), (0.75, 0.25), (1.0 / 3.0, 2.0 / 3.0))


def stage_plane(kind, src, base, plane, put):
    old, new = WEIGHTS[kind]
    row = lax.broadcasted_iota(jnp.int32, (8, 128), 0)
    first, last = row == 0, row == 7
    tile = 2 * plane
    core = [[src[c, tile + h] for h in range(2)] for c in range(3)]
    wind = [[core[c][h] * (new * HALF) for h in range(2)] for c in range(3)]
    for c in range(3):
        a, b = core[c]
        ra, rb = pltpu.roll(a, 1, 0), pltpu.roll(b, 1, 0)
        la, lb = pltpu.roll(a, 7, 0), pltpu.roll(b, 7, 0)
        before = (jnp.where(first, rb, ra), jnp.where(first, ra, rb))
        after = (jnp.where(last, lb, la), jnp.where(last, la, lb))
        for h in range(2):
            v = core[c][h]
            xm, xp = pltpu.roll(v, 1, 1), pltpu.roll(v, 127, 1)
            zm, zp = src[c, tile + h - 2], src[c, tile + h + 2]
            near = (xp + xm) + (after[h] + before[h]) + (zp + zm)
            advect = wind[0][h] * (xp - xm) + wind[1][h] * (after[h] - before[h]) + wind[2][h] * (zp - zm)
            out = (new * KEEP) * v + ((new * NEAR) * near - advect)
            if kind:
                out = out + old * base[c, tile + h]
            put(c, h, out)


def kernel(states, rate_in, out, rate, w0, w1, w2, w3, w4, w5, jump, got, total, tots, path,
           load_sem, halo_send, halo_recv, up_send, up_recv, row_send, row_recv, down_send, down_recv, own_sem):
    tm, gz = lax.axis_index("tm"), lax.axis_index("gz")
    zi, row = tm & (RING - 1), tm // RING
    above, below = (gz + 1) & (SLABS - 1), (gz + SLABS - 1) & (SLABS - 1)
    far = gz & 1
    start = row * RING

    load = pltpu.make_async_copy(states, w0.at[:, pl.ds(2 * WIDE, 2 * OWN)], load_sem.at[0])
    load.start()
    load_rate = pltpu.make_async_copy(rate_in, rate, load_sem.at[1])
    load_rate.start()
    barrier = pltpu.get_barrier_semaphore()
    for peer in (above, below):
        pl.semaphore_signal(barrier, inc=1, device_id={"gz": peer}, device_id_type=MESH)
    for q in range(1, RING):
        pl.semaphore_signal(barrier, inc=1, device_id={"tm": start + ((zi + q) & (RING - 1))}, device_id_type=MESH)

    def greet(q, carry):
        pl.semaphore_signal(barrier, inc=1, device_id={"tm": q * RING + zi}, device_id_type=MESH)
        return carry

    lax.fori_loop(0, row, greet, 0)
    def halo(upper, outer):
        planes = WIDE - NEXT if outer else NEXT
        if upper:
            source, target = (NEXT if outer else 0), OWN + WIDE + (NEXT if outer else 0)
        else:
            source, target = OWN - (WIDE if outer else NEXT), (0 if outer else WIDE - NEXT)
        return pltpu.make_async_remote_copy(
            w0.at[:, pl.ds(2 * (WIDE + source), 2 * planes)], w0.at[:, pl.ds(2 * target, 2 * planes)],
            halo_send.at[upper, outer], halo_recv.at[upper, outer],
            device_id={"gz": below if upper else above}, device_id_type=MESH)

    @pl.when(tm == 0)
    def _():
        pltpu.make_async_copy(states, out, own_sem.at[0]).start()

    works = (w0, w1, w2, w3, w4, w5)
    keep_own = jnp.where(tm == 0, 0.0, 1.0)

    def stages(first_plane, count, at_once, ks=range(1, 7)):
        for k in ks:
            src, base = works[k - 1], works[3 * ((k - 1) // 3)]
            kind = (k - 1) % 3
            begin = first_plane(k)

            def one_plane(plane, k, src, base, kind):
                if k < 6:
                    def put(c, h, value):
                        works[k][c, 2 * plane + h] = value
                else:
                    damp = [jnp.exp(rate[2 * (plane - WIDE) + h] * (-1.0 / SLICES)) * keep_own for h in range(2)]

                    def put(c, h, value):
                        jump[c, 2 * (plane - WIDE) + h] = value - damp[h] * w0[c, 2 * plane + h]

                stage_plane(kind, src, base, plane, put)

            def turn(i, carry, k=k, src=src, base=base, kind=kind, begin=begin):
                for j in range(at_once[k - 1]):
                    one_plane(begin + at_once[k - 1] * i + j, k, src, base, kind)
                return carry

            turns = count(k) // at_once[k - 1]
            if turns == 1:
                turn(0, 0)
            else:
                lax.fori_loop(0, turns, turn, 0)

    def tile_of(group, k):
        if group == 2:
            return k + jnp.where(k >= 4, 4 + 12 * far, 28 - 28 * far)
        return k + (12, 20 - 16 * far, None, 24 * far)[group]

    def send_up(group):
        for q in (4, 3, 5, 2, 6, 1, 7):
            peer = ((zi + q) & (RING - 1))
            pltpu.make_async_remote_copy(
                jump.at[:, tile_of(group, peer)], got.at[group, zi], up_send.at[group], up_recv.at[group],
                device_id={"tm": start + peer}, device_id_type=MESH).start()

    def all_of(buf, send, recv):
        return pltpu.make_async_remote_copy(
            buf.at[pl.ds(0, RING - 1)], buf.at[pl.ds(0, RING - 1)], send, recv,
            device_id={"tm": tm}, device_id_type=MESH)

    def damp_of(group):
        return jnp.exp(rate[tile_of(group, zi)] * (-1.0 / SLICES))

    def sum_row(group):
        all_of(got.at[group], up_send.at[group], up_recv.at[group]).wait_recv()
        mine = tile_of(group, zi)
        for c in range(3):
            got[group, zi, c] = jump[c, mine]
        damp = damp_of(group)
        acc = [got[group, 0, c] for c in range(3)]
        for z in range(1, RING):
            acc = [damp * acc[c] + got[group, z, c] for c in range(3)]
        for c in range(3):
            total[group, c] = acc[c]

        def tell(later, carry):
            pltpu.make_async_remote_copy(
                total.at[group], tots.at[group, row], row_send.at[group, later], row_recv.at[group, row],
                device_id={"tm": later * RING + zi}, device_id_type=MESH).start()
            return carry

        lax.fori_loop(0, ROWS - 1 - row, lambda i, carry: tell(ROWS - 1 - i, carry), 0)

    def send_down(group):
        damp = damp_of(group)
        eighth = damp * damp
        eighth = eighth * eighth
        eighth = eighth * eighth

        def add(q, carry):
            pltpu.make_async_remote_copy(
                total.at[group], tots.at[group, q], row_send.at[group, q], row_recv.at[group, q],
                device_id={"tm": q * RING + zi}, device_id_type=MESH).wait_recv()
            return tuple(eighth * carry[c] + tots[group, q, c] for c in range(3))

        acc = lax.fori_loop(0, row, add, tuple(jnp.zeros((8, 128), jnp.float32) for _ in range(3)))
        for z in range(RING):
            for c in range(3):
                path[group, z, c] = acc[c]
            if z < RING - 1:
                acc = [damp * acc[c] + got[group, z, c] for c in range(3)]
        mine = tile_of(group, zi)
        for q in (4, 3, 5, 2, 6, 1, 7):
            peer = ((zi + q) & (RING - 1))

            @pl.when(start + peer > 0)
            def _():
                pltpu.make_async_remote_copy(
                    path.at[group, peer], out.at[:, mine], down_send.at[group, q], down_recv.at[group, q],
                    device_id={"tm": start + peer}, device_id_type=MESH).start()

        @pl.when(tm > 0)
        def _():
            pltpu.make_async_copy(path.at[group, zi], out.at[:, mine], own_sem.at[group]).start()

    load.wait()
    load_rate.wait()
    inside = lambda ks: stages(lambda k: WIDE + k, lambda k: OWN - 2 * k, (7, 6, 5, 8, 6, 4), ks)
    inside(range(1, 3))
    pl.semaphore_wait(barrier, 2 + (RING - 1) + (ROWS - 1 - row))

    for upper in (0, 1):
        @pl.when(upper == 1 - far)
        def _(upper=upper):
            halo(1 - upper, 0).start()
            halo(upper, 0).start()
            halo(upper, 1).start()
            halo(1 - upper, 1).start()

    inside(range(3, 7))
    send_up(0)

    def halo_wait(upper, outers):
        for choice in (0, 1):
            @pl.when(upper == choice)
            def _(choice=choice):
                for outer in outers:
                    halo(choice, outer).wait_recv()

    def side(upper, skip, planes):
        stages(lambda k: jnp.where(upper == 1, SPAN - WIDE + skip - k, WIDE - skip - planes + k), lambda k: planes, (planes,) * 6)

    near_upper, far_upper = 1 - far, far
    halo_wait(near_upper, (0, 1))
    side(near_upper, 0, WIDE)
    send_up(1)
    halo_wait(far_upper, (0,))
    side(far_upper, 0, NEXT)
    send_up(2)
    sum_row(0)
    halo_wait(far_upper, (1,))
    side(far_upper, NEXT, WIDE - NEXT)
    send_up(3)
    sum_row(1)
    send_down(0)
    sum_row(2)
    send_down(1)
    sum_row(3)
    send_down(2)
    send_down(3)

    for group in range(GROUPS):
        mine = tile_of(group, zi)
        all_of(got.at[group], up_send.at[group], up_recv.at[group]).wait_send()

        def told(later, carry, group=group):
            pltpu.make_async_remote_copy(
                total.at[group], tots.at[group, row], row_send.at[group, later], row_recv.at[group, row],
                device_id={"tm": later * RING + zi}, device_id_type=MESH).wait_send()
            return carry

        lax.fori_loop(row + 1, ROWS, told, 0)
        for q in range(1, RING):
            peer, source = ((zi + q) & (RING - 1)), ((zi + RING - q) & (RING - 1))

            @pl.when(start + peer > 0)
            def _():
                pltpu.make_async_remote_copy(
                    path.at[group, peer], out.at[:, mine], down_send.at[group, q], down_recv.at[group, q],
                    device_id={"tm": start + peer}, device_id_type=MESH).wait_send()

            @pl.when(tm > 0)
            def _():
                pltpu.make_async_remote_copy(
                    path.at[group, zi], out.at[:, tile_of(group, source)], down_send.at[group, q], down_recv.at[group, q],
                    device_id={"tm": start + source}, device_id_type=MESH).wait_recv()

        @pl.when(tm > 0)
        def _():
            pltpu.make_async_copy(path.at[group, zi], out.at[:, mine], own_sem.at[group]).wait()

    @pl.when(tm == 0)
    def _():
        pltpu.make_async_copy(states, out, own_sem.at[0]).wait()

    for upper in (0, 1):
        for outer in (0, 1):
            halo(upper, outer).wait_send()


def shards(states, rate):
    f32 = jnp.float32
    work = pltpu.VMEM((3, 2 * SPAN, 8, 128), f32)
    dma = pltpu.SemaphoreType.DMA
    out = pl.pallas_call(
        kernel,
        out_shape=jax.ShapeDtypeStruct((3, 2 * OWN, 8, 128), f32),
        in_specs=[pl.BlockSpec(memory_space=pltpu.HBM), pl.BlockSpec(memory_space=pltpu.HBM)],
        out_specs=pl.BlockSpec(memory_space=pl.ANY),
        scratch_shapes=[pltpu.VMEM((2 * OWN, 8, 128), f32)] + [work] * 6 + [
            pltpu.VMEM((3, 2 * OWN, 8, 128), f32),
            pltpu.VMEM((GROUPS, RING, 3, 8, 128), f32),
            pltpu.VMEM((GROUPS, 3, 8, 128), f32),
            pltpu.VMEM((GROUPS, ROWS, 3, 8, 128), f32),
            pltpu.VMEM((GROUPS, RING, 3, 8, 128), f32),
            dma((2,)), dma((2, 2)), dma((2, 2)), dma((GROUPS,)), dma((GROUPS,)),
            dma((GROUPS, ROWS)), dma((GROUPS, ROWS)), dma((GROUPS, RING)), dma((GROUPS, RING)), dma((GROUPS,)),
        ],
        compiler_params=pltpu.CompilerParams(collective_id=0, has_side_effects=True, vmem_limit_bytes=32 * 1024 * 1024),
    )(pltpu.with_memory_space_constraint(states.reshape(3, 2 * OWN, 8, 128), pltpu.HBM), pltpu.with_memory_space_constraint(rate.reshape(2 * OWN, 8, 128), pltpu.HBM))
    return out.reshape(1, 3, OWN, 16, 128)


def solution(mesh):
    return jax.shard_map(
        shards,
        mesh=mesh,
        in_specs=(P("tm", None, "gz", None, None), P("gz", None, None)),
        out_specs=P("tm", None, "gz", None, None),
        check_vma=False,
    )
```

```python
import jax
import jax.numpy as jnp
from jax import lax
from jax.experimental import pallas as pl
from jax.experimental.pallas import tpu as pltpu
from jax.sharding import PartitionSpec as P

STEPS = 2
VISCOSITY = 0.05
TIME_STEP = 0.2
SLICES = 64
RING = 8
ROWS = 8
SLABS = 4
WIDE = 3 * STEPS
NEXT = 2
OWN = 16
SPAN = OWN + 2 * WIDE
GROUPS = 4
MESH = pl.DeviceIdType.MESH

KEEP = 1.0 - 6.0 * VISCOSITY * TIME_STEP
NEAR = VISCOSITY * TIME_STEP
HALF = 0.5 * TIME_STEP
WEIGHTS = ((0.0, 1.0), (0.75, 0.25), (1.0 / 3.0, 2.0 / 3.0))


def stage_plane(kind, src, base, plane, put):
    old, new = WEIGHTS[kind]
    row = lax.broadcasted_iota(jnp.int32, (8, 128), 0)
    first, last = row == 0, row == 7
    tile = 2 * plane
    core = [[src[c, tile + h] for h in range(2)] for c in range(3)]
    wind = [[core[c][h] * (new * HALF) for h in range(2)] for c in range(3)]
    for c in range(3):
        a, b = core[c]
        ra, rb = pltpu.roll(a, 1, 0), pltpu.roll(b, 1, 0)
        la, lb = pltpu.roll(a, 7, 0), pltpu.roll(b, 7, 0)
        before = (jnp.where(first, rb, ra), jnp.where(first, ra, rb))
        after = (jnp.where(last, lb, la), jnp.where(last, la, lb))
        for h in range(2):
            v = core[c][h]
            xm, xp = pltpu.roll(v, 1, 1), pltpu.roll(v, 127, 1)
            zm, zp = src[c, tile + h - 2], src[c, tile + h + 2]
            near = (xp + xm) + (after[h] + before[h]) + (zp + zm)
            advect = wind[0][h] * (xp - xm) + wind[1][h] * (after[h] - before[h]) + wind[2][h] * (zp - zm)
            out = (new * KEEP) * v + ((new * NEAR) * near - advect)
            if kind:
                out = out + old * base[c, tile + h]
            put(c, h, out)


def kernel(states, rate_in, out, rate, w0, w1, w2, w3, w4, w5, jump, got, total, tots, path,
           load_sem, halo_send, halo_recv, up_send, up_recv, row_send, row_recv, down_send, down_recv, own_sem):
    tm, gz = lax.axis_index("tm"), lax.axis_index("gz")
    zi, row = tm & (RING - 1), tm // RING
    above, below = (gz + 1) & (SLABS - 1), (gz + SLABS - 1) & (SLABS - 1)
    far = gz & 1
    start = row * RING

    load = pltpu.make_async_copy(states, w0.at[:, pl.ds(2 * WIDE, 2 * OWN)], load_sem.at[0])
    load.start()
    load_rate = pltpu.make_async_copy(rate_in, rate, load_sem.at[1])
    load_rate.start()
    barrier = pltpu.get_barrier_semaphore()
    for peer in (above, below):
        pl.semaphore_signal(barrier, inc=1, device_id={"gz": peer}, device_id_type=MESH)
    for q in range(1, RING):
        pl.semaphore_signal(barrier, inc=1, device_id={"tm": start + ((zi + q) & (RING - 1))}, device_id_type=MESH)

    def greet(q, carry):
        pl.semaphore_signal(barrier, inc=1, device_id={"tm": q * RING + zi}, device_id_type=MESH)
        return carry

    lax.fori_loop(0, row, greet, 0)
    def halo(upper, outer):
        planes = WIDE - NEXT if outer else NEXT
        if upper:
            source, target = (NEXT if outer else 0), OWN + WIDE + (NEXT if outer else 0)
        else:
            source, target = OWN - (WIDE if outer else NEXT), (0 if outer else WIDE - NEXT)
        return pltpu.make_async_remote_copy(
            w0.at[:, pl.ds(2 * (WIDE + source), 2 * planes)], w0.at[:, pl.ds(2 * target, 2 * planes)],
            halo_send.at[upper, outer], halo_recv.at[upper, outer],
            device_id={"gz": below if upper else above}, device_id_type=MESH)

    @pl.when(tm == 0)
    def _():
        pltpu.make_async_copy(states, out, own_sem.at[0]).start()

    works = (w0, w1, w2, w3, w4, w5)
    keep_own = jnp.where(tm == 0, 0.0, 1.0)
    busy = tm < SLICES - 1

    def stages(first_plane, count, at_once, ks=range(1, 7)):
        for k in ks:
            src, base = works[k - 1], works[3 * ((k - 1) // 3)]
            kind = (k - 1) % 3
            begin = first_plane(k)

            def one_plane(plane, k, src, base, kind):
                if k < 6:
                    def put(c, h, value):
                        works[k][c, 2 * plane + h] = value
                else:
                    damp = [jnp.exp(rate[2 * (plane - WIDE) + h] * (-1.0 / SLICES)) * keep_own for h in range(2)]

                    def put(c, h, value):
                        jump[c, 2 * (plane - WIDE) + h] = value - damp[h] * w0[c, 2 * plane + h]

                stage_plane(kind, src, base, plane, put)

            def turn(i, carry, k=k, src=src, base=base, kind=kind, begin=begin):
                for j in range(at_once[k - 1]):
                    one_plane(begin + at_once[k - 1] * i + j, k, src, base, kind)
                return carry

            turns = count(k) // at_once[k - 1]
            if turns == 1:
                turn(0, 0)
            else:
                lax.fori_loop(0, turns, turn, 0)

    def tile_of(group, k):
        if group == 2:
            return k + jnp.where(k >= 4, 4 + 12 * far, 28 - 28 * far)
        return k + (12, 20 - 16 * far, None, 24 * far)[group]

    def send_up(group):
        for q in (4, 3, 5, 2, 6, 1, 7):
            peer = ((zi + q) & (RING - 1))
            pltpu.make_async_remote_copy(
                jump.at[:, tile_of(group, peer)], got.at[group, zi], up_send.at[group], up_recv.at[group],
                device_id={"tm": start + peer}, device_id_type=MESH).start()

    def all_of(buf, send, recv, count=RING - 1):
        return pltpu.make_async_remote_copy(
            buf.at[pl.ds(0, count)], buf.at[pl.ds(0, count)], send, recv,
            device_id={"tm": tm}, device_id_type=MESH)

    def damp_of(group):
        return jnp.exp(rate[tile_of(group, zi)] * (-1.0 / SLICES))

    def sum_row(group):
        short = (row == ROWS - 1) & (zi < RING - 1)

        @pl.when(short)
        def _():
            all_of(got.at[group], up_send.at[group], up_recv.at[group], RING - 2).wait_recv()

        @pl.when(jnp.logical_not(short))
        def _():
            all_of(got.at[group], up_send.at[group], up_recv.at[group]).wait_recv()

        @pl.when(busy)
        def _():
            mine = tile_of(group, zi)
            for c in range(3):
                got[group, zi, c] = jump[c, mine]

        @pl.when(row < ROWS - 1)
        def _():
            damp = damp_of(group)
            acc = [got[group, 0, c] for c in range(3)]
            for z in range(1, RING):
                acc = [damp * acc[c] + got[group, z, c] for c in range(3)]
            for c in range(3):
                total[group, c] = acc[c]

        def tell(later, carry):
            pltpu.make_async_remote_copy(
                total.at[group], tots.at[group, row], row_send.at[group, later], row_recv.at[group, row],
                device_id={"tm": later * RING + zi}, device_id_type=MESH).start()
            return carry

        lax.fori_loop(0, ROWS - 1 - row, lambda i, carry: tell(ROWS - 1 - i, carry), 0)

    def send_down(group):
        damp = damp_of(group)
        eighth = damp * damp
        eighth = eighth * eighth
        eighth = eighth * eighth

        def add(q, carry):
            pltpu.make_async_remote_copy(
                total.at[group], tots.at[group, q], row_send.at[group, q], row_recv.at[group, q],
                device_id={"tm": q * RING + zi}, device_id_type=MESH).wait_recv()
            return tuple(eighth * carry[c] + tots[group, q, c] for c in range(3))

        acc = lax.fori_loop(0, row, add, tuple(jnp.zeros((8, 128), jnp.float32) for _ in range(3)))
        for z in range(RING):
            for c in range(3):
                path[group, z, c] = acc[c]
            if z < RING - 1:
                acc = [damp * acc[c] + got[group, z, c] for c in range(3)]
        mine = tile_of(group, zi)
        for q in (4, 3, 5, 2, 6, 1, 7):
            peer = ((zi + q) & (RING - 1))

            @pl.when(start + peer > 0)
            def _():
                pltpu.make_async_remote_copy(
                    path.at[group, peer], out.at[:, mine], down_send.at[group, q], down_recv.at[group, q],
                    device_id={"tm": start + peer}, device_id_type=MESH).start()

        @pl.when(tm > 0)
        def _():
            pltpu.make_async_copy(path.at[group, zi], out.at[:, mine], own_sem.at[group]).start()

    def halo_wait(upper, outers):
        for choice in (0, 1):
            @pl.when(upper == choice)
            def _(choice=choice):
                for outer in outers:
                    halo(choice, outer).wait_recv()

    def side(upper, skip, planes):
        stages(lambda k: jnp.where(upper == 1, SPAN - WIDE + skip - k, WIDE - skip - planes + k), lambda k: planes, (planes,) * 6)

    load.wait()
    load_rate.wait()
    inside = lambda ks: stages(lambda k: WIDE + k, lambda k: OWN - 2 * k, (7, 6, 5, 8, 6, 4), ks)
    near_upper, far_upper = 1 - far, far

    @pl.when(busy)
    def _():
        inside(range(1, 3))

    pl.semaphore_wait(barrier, 2 + (RING - 1) + (ROWS - 1 - row))

    @pl.when(busy)
    def _():
        for upper in (0, 1):
            @pl.when(upper == 1 - far)
            def _(upper=upper):
                halo(1 - upper, 0).start()
                halo(upper, 0).start()
                halo(upper, 1).start()
                halo(1 - upper, 1).start()

        inside(range(3, 7))
        send_up(0)
        halo_wait(near_upper, (0, 1))
        side(near_upper, 0, WIDE)
        send_up(1)
        halo_wait(far_upper, (0,))
        side(far_upper, 0, NEXT)
        send_up(2)

    sum_row(0)

    @pl.when(busy)
    def _():
        halo_wait(far_upper, (1,))
        side(far_upper, NEXT, WIDE - NEXT)
        send_up(3)

    sum_row(1)
    send_down(0)
    sum_row(2)
    send_down(1)
    sum_row(3)
    send_down(2)
    send_down(3)

    for group in range(GROUPS):
        mine = tile_of(group, zi)
        @pl.when(busy)
        def _(group=group):
            all_of(got.at[group], up_send.at[group], up_recv.at[group]).wait_send()


        def told(later, carry, group=group):
            pltpu.make_async_remote_copy(
                total.at[group], tots.at[group, row], row_send.at[group, later], row_recv.at[group, row],
                device_id={"tm": later * RING + zi}, device_id_type=MESH).wait_send()
            return carry

        lax.fori_loop(row + 1, ROWS, told, 0)
        for q in range(1, RING):
            peer, source = ((zi + q) & (RING - 1)), ((zi + RING - q) & (RING - 1))

            @pl.when(start + peer > 0)
            def _():
                pltpu.make_async_remote_copy(
                    path.at[group, peer], out.at[:, mine], down_send.at[group, q], down_recv.at[group, q],
                    device_id={"tm": start + peer}, device_id_type=MESH).wait_send()

            @pl.when(tm > 0)
            def _():
                pltpu.make_async_remote_copy(
                    path.at[group, zi], out.at[:, tile_of(group, source)], down_send.at[group, q], down_recv.at[group, q],
                    device_id={"tm": start + source}, device_id_type=MESH).wait_recv()

        @pl.when(tm > 0)
        def _():
            pltpu.make_async_copy(path.at[group, zi], out.at[:, mine], own_sem.at[group]).wait()

    @pl.when(tm == 0)
    def _():
        pltpu.make_async_copy(states, out, own_sem.at[0]).wait()

    @pl.when(busy)
    def _():
        for upper in (0, 1):
            for outer in (0, 1):
                halo(upper, outer).wait_send()


def shards(states, rate):
    f32 = jnp.float32
    work = pltpu.VMEM((3, 2 * SPAN, 8, 128), f32)
    dma = pltpu.SemaphoreType.DMA
    out = pl.pallas_call(
        kernel,
        out_shape=jax.ShapeDtypeStruct((3, 2 * OWN, 8, 128), f32),
        in_specs=[pl.BlockSpec(memory_space=pltpu.HBM), pl.BlockSpec(memory_space=pltpu.HBM)],
        out_specs=pl.BlockSpec(memory_space=pl.ANY),
        scratch_shapes=[pltpu.VMEM((2 * OWN, 8, 128), f32)] + [work] * 6 + [
            pltpu.VMEM((3, 2 * OWN, 8, 128), f32),
            pltpu.VMEM((GROUPS, RING, 3, 8, 128), f32),
            pltpu.VMEM((GROUPS, 3, 8, 128), f32),
            pltpu.VMEM((GROUPS, ROWS, 3, 8, 128), f32),
            pltpu.VMEM((GROUPS, RING, 3, 8, 128), f32),
            dma((2,)), dma((2, 2)), dma((2, 2)), dma((GROUPS,)), dma((GROUPS,)),
            dma((GROUPS, ROWS)), dma((GROUPS, ROWS)), dma((GROUPS, RING)), dma((GROUPS, RING)), dma((GROUPS,)),
        ],
        compiler_params=pltpu.CompilerParams(collective_id=0, has_side_effects=True, vmem_limit_bytes=32 * 1024 * 1024),
    )(pltpu.with_memory_space_constraint(states.reshape(3, 2 * OWN, 8, 128), pltpu.HBM), pltpu.with_memory_space_constraint(rate.reshape(2 * OWN, 8, 128), pltpu.HBM))
    return out.reshape(1, 3, OWN, 16, 128)


def solution(mesh):
    return jax.shard_map(
        shards,
        mesh=mesh,
        in_specs=(P("tm", None, "gz", None, None), P("gz", None, None)),
        out_specs=P("tm", None, "gz", None, None),
        check_vma=False,
    )
```

```python
import jax
import jax.numpy as jnp
from jax import lax
from jax.experimental import pallas as pl
from jax.experimental.pallas import tpu as pltpu
from jax.sharding import PartitionSpec as P

STEPS = 2
VISCOSITY = 0.05
TIME_STEP = 0.2
SLICES = 64
RING = 8
ROWS = 8
SLABS = 4
WIDE = 3 * STEPS
NEXT = 2
OWN = 16
SPAN = OWN + 2 * WIDE
GROUPS = 4
MESH = pl.DeviceIdType.MESH

KEEP = 1.0 - 6.0 * VISCOSITY * TIME_STEP
NEAR = VISCOSITY * TIME_STEP
HALF = 0.5 * TIME_STEP
WEIGHTS = ((0.0, 1.0), (0.75, 0.25), (1.0 / 3.0, 2.0 / 3.0))


def stage_plane(kind, src, base, plane, put):
    old, new = WEIGHTS[kind]
    row = lax.broadcasted_iota(jnp.int32, (8, 128), 0)
    first, last = row == 0, row == 7
    tile = 2 * plane
    core = [[src[c, tile + h] for h in range(2)] for c in range(3)]
    wind = [[core[c][h] * (new * HALF) for h in range(2)] for c in range(3)]
    for c in range(3):
        a, b = core[c]
        ra, rb = pltpu.roll(a, 1, 0), pltpu.roll(b, 1, 0)
        la, lb = pltpu.roll(a, 7, 0), pltpu.roll(b, 7, 0)
        before = (jnp.where(first, rb, ra), jnp.where(first, ra, rb))
        after = (jnp.where(last, lb, la), jnp.where(last, la, lb))
        for h in range(2):
            v = core[c][h]
            xm, xp = pltpu.roll(v, 1, 1), pltpu.roll(v, 127, 1)
            zm, zp = src[c, tile + h - 2], src[c, tile + h + 2]
            near = (xp + xm) + (after[h] + before[h]) + (zp + zm)
            advect = wind[0][h] * (xp - xm) + wind[1][h] * (after[h] - before[h]) + wind[2][h] * (zp - zm)
            out = (new * KEEP) * v + ((new * NEAR) * near - advect)
            if kind:
                out = out + old * base[c, tile + h]
            put(c, h, out)


def kernel(states, rate_in, out, rate, w0, w1, w2, w3, w4, w5, jump, got, total, tots, path,
           load_sem, halo_send, halo_recv, up_send, up_recv, row_send, row_recv, down_send, down_recv, own_sem):
    tm, gz = lax.axis_index("tm"), lax.axis_index("gz")
    zi, row = tm & (RING - 1), tm // RING
    above, below = (gz + 1) & (SLABS - 1), (gz + SLABS - 1) & (SLABS - 1)
    far = gz & 1
    start = row * RING

    load = pltpu.make_async_copy(states, w0.at[:, pl.ds(2 * WIDE, 2 * OWN)], load_sem.at[0])
    load.start()
    load_rate = pltpu.make_async_copy(rate_in, rate, load_sem.at[1])
    load_rate.start()
    barrier = pltpu.get_barrier_semaphore()
    for peer in (above, below):
        pl.semaphore_signal(barrier, inc=1, device_id={"gz": peer}, device_id_type=MESH)
    for q in range(1, RING):
        pl.semaphore_signal(barrier, inc=1, device_id={"tm": start + ((zi + q) & (RING - 1))}, device_id_type=MESH)

    def greet(q, carry):
        pl.semaphore_signal(barrier, inc=1, device_id={"tm": q * RING + zi}, device_id_type=MESH)
        return carry

    lax.fori_loop(0, row, greet, 0)
    def halo(upper, outer):
        planes = WIDE - NEXT if outer else NEXT
        if upper:
            source, target = (NEXT if outer else 0), OWN + WIDE + (NEXT if outer else 0)
        else:
            source, target = OWN - (WIDE if outer else NEXT), (0 if outer else WIDE - NEXT)
        return pltpu.make_async_remote_copy(
            w0.at[:, pl.ds(2 * (WIDE + source), 2 * planes)], w0.at[:, pl.ds(2 * target, 2 * planes)],
            halo_send.at[upper, outer], halo_recv.at[upper, outer],
            device_id={"gz": below if upper else above}, device_id_type=MESH)

    @pl.when(tm == 0)
    def _():
        pltpu.make_async_copy(states, out, own_sem.at[0]).start()

    works = (w0, w1, w2, w3, w4, w5)
    keep_own = jnp.where(tm == 0, 0.0, 1.0)
    busy = tm < SLICES - 1

    def stages(first_plane, count, at_once, ks=range(1, 7)):
        for k in ks:
            src, base = works[k - 1], works[3 * ((k - 1) // 3)]
            kind = (k - 1) % 3
            begin = first_plane(k)

            def one_plane(plane, k, src, base, kind):
                if k < 6:
                    def put(c, h, value):
                        works[k][c, 2 * plane + h] = value
                else:
                    damp = [jnp.exp(rate[2 * (plane - WIDE) + h] * (-1.0 / SLICES)) * keep_own for h in range(2)]

                    def put(c, h, value):
                        jump[c, 2 * (plane - WIDE) + h] = value - damp[h] * w0[c, 2 * plane + h]

                stage_plane(kind, src, base, plane, put)

            def turn(i, carry, k=k, src=src, base=base, kind=kind, begin=begin):
                for j in range(at_once[k - 1]):
                    one_plane(begin + at_once[k - 1] * i + j, k, src, base, kind)
                return carry

            turns = count(k) // at_once[k - 1]
            if turns == 1:
                turn(0, 0)
            else:
                lax.fori_loop(0, turns, turn, 0)

    def tile_of(group, k):
        if group == 2:
            return k + jnp.where(k >= 4, 4 + 12 * far, 28 - 28 * far)
        return k + (12, 20 - 16 * far, None, 24 * far)[group]

    def send_up(group):
        for q in (4, 3, 5, 2, 6, 1, 7):
            peer = ((zi + q) & (RING - 1))
            pltpu.make_async_remote_copy(
                jump.at[:, tile_of(group, peer)], got.at[group, zi], up_send.at[group], up_recv.at[group],
                device_id={"tm": start + peer}, device_id_type=MESH).start()

    def all_of(buf, send, recv, count=RING - 1):
        return pltpu.make_async_remote_copy(
            buf.at[pl.ds(0, count)], buf.at[pl.ds(0, count)], send, recv,
            device_id={"tm": tm}, device_id_type=MESH)

    def damp_of(group):
        return jnp.exp(rate[tile_of(group, zi)] * (-1.0 / SLICES))

    def sum_row(group):
        short = (row == ROWS - 1) & (zi < RING - 1)

        @pl.when(short)
        def _():
            all_of(got.at[group], up_send.at[group], up_recv.at[group], RING - 2).wait_recv()

        @pl.when(jnp.logical_not(short))
        def _():
            all_of(got.at[group], up_send.at[group], up_recv.at[group]).wait_recv()

        @pl.when(busy)
        def _():
            mine = tile_of(group, zi)
            for c in range(3):
                got[group, zi, c] = jump[c, mine]

        @pl.when(row < ROWS - 1)
        def _():
            damp = damp_of(group)
            acc = [got[group, 0, c] for c in range(3)]
            for z in range(1, RING):
                acc = [damp * acc[c] + got[group, z, c] for c in range(3)]
            for c in range(3):
                total[group, c] = acc[c]

        for ahead in range(ROWS - 1, 0, -1):
            @pl.when(row + ahead < ROWS)
            def _(ahead=ahead):
                pltpu.make_async_remote_copy(
                    total.at[group], tots.at[group, row], row_send.at[group, ahead], row_recv.at[group, row],
                    device_id={"tm": (row + ahead) * RING + zi}, device_id_type=MESH).start()

    def send_down(group):
        damp = damp_of(group)
        eighth = damp * damp
        eighth = eighth * eighth
        eighth = eighth * eighth

        def add(q, carry):
            pltpu.make_async_remote_copy(
                total.at[group], tots.at[group, q], row_send.at[group, q], row_recv.at[group, q],
                device_id={"tm": q * RING + zi}, device_id_type=MESH).wait_recv()
            return tuple(eighth * carry[c] + tots[group, q, c] for c in range(3))

        acc = lax.fori_loop(0, row, add, tuple(jnp.zeros((8, 128), jnp.float32) for _ in range(3)))
        for z in range(RING):
            for c in range(3):
                path[group, z, c] = acc[c]
            if z < RING - 1:
                acc = [damp * acc[c] + got[group, z, c] for c in range(3)]
        mine = tile_of(group, zi)
        for q in (4, 5, 3, 6, 2, 7, 1):
            peer = ((zi + q) & (RING - 1))

            @pl.when(start + peer > 0)
            def _():
                pltpu.make_async_remote_copy(
                    path.at[group, peer], out.at[:, mine], down_send.at[group, q], down_recv.at[group, q],
                    device_id={"tm": start + peer}, device_id_type=MESH).start()

        @pl.when(tm > 0)
        def _():
            pltpu.make_async_copy(path.at[group, zi], out.at[:, mine], own_sem.at[group]).start()

    def halo_wait(upper, outers):
        for choice in (0, 1):
            @pl.when(upper == choice)
            def _(choice=choice):
                for outer in outers:
                    halo(choice, outer).wait_recv()

    def side(upper, skip, planes):
        stages(lambda k: jnp.where(upper == 1, SPAN - WIDE + skip - k, WIDE - skip - planes + k), lambda k: planes, (planes,) * 6)

    load.wait()
    inside = lambda ks: stages(lambda k: WIDE + k, lambda k: OWN - 2 * k, (7, 6, 5, 8, 6, 4), ks)
    near_upper, far_upper = 1 - far, far

    @pl.when(busy)
    def _():
        inside(range(1, 3))

    pl.semaphore_wait(barrier, 2 + (RING - 1) + (ROWS - 1 - row))
    load_rate.wait()

    @pl.when(busy)
    def _():
        for upper in (0, 1):
            @pl.when(upper == 1 - far)
            def _(upper=upper):
                halo(1 - upper, 0).start()
                halo(upper, 0).start()
                halo(upper, 1).start()
                halo(1 - upper, 1).start()

        inside(range(3, 7))
        send_up(0)
        halo_wait(near_upper, (0, 1))
        side(near_upper, 0, WIDE)
        send_up(1)
        halo_wait(far_upper, (0,))
        side(far_upper, 0, NEXT)
        send_up(2)

    sum_row(0)

    @pl.when(busy)
    def _():
        halo_wait(far_upper, (1,))
        side(far_upper, NEXT, WIDE - NEXT)
        send_up(3)

    sum_row(1)
    send_down(0)
    sum_row(2)
    send_down(1)
    sum_row(3)
    send_down(2)
    send_down(3)

    for group in range(GROUPS):
        mine = tile_of(group, zi)
        @pl.when(busy)
        def _(group=group):
            all_of(got.at[group], up_send.at[group], up_recv.at[group]).wait_send()


        for ahead in range(1, ROWS):
            @pl.when(row + ahead < ROWS)
            def _(ahead=ahead, group=group):
                pltpu.make_async_remote_copy(
                    total.at[group], tots.at[group, row], row_send.at[group, ahead], row_recv.at[group, row],
                    device_id={"tm": (row + ahead) * RING + zi}, device_id_type=MESH).wait_send()

        for q in range(1, RING):
            peer, source = ((zi + q) & (RING - 1)), ((zi + RING - q) & (RING - 1))

            @pl.when(start + peer > 0)
            def _():
                pltpu.make_async_remote_copy(
                    path.at[group, peer], out.at[:, mine], down_send.at[group, q], down_recv.at[group, q],
                    device_id={"tm": start + peer}, device_id_type=MESH).wait_send()

            @pl.when(tm > 0)
            def _():
                pltpu.make_async_remote_copy(
                    path.at[group, zi], out.at[:, tile_of(group, source)], down_send.at[group, q], down_recv.at[group, q],
                    device_id={"tm": start + source}, device_id_type=MESH).wait_recv()

        @pl.when(tm > 0)
        def _():
            pltpu.make_async_copy(path.at[group, zi], out.at[:, mine], own_sem.at[group]).wait()

    @pl.when(tm == 0)
    def _():
        pltpu.make_async_copy(states, out, own_sem.at[0]).wait()

    @pl.when(busy)
    def _():
        for upper in (0, 1):
            for outer in (0, 1):
                halo(upper, outer).wait_send()


def shards(states, rate):
    f32 = jnp.float32
    work = pltpu.VMEM((3, 2 * SPAN, 8, 128), f32)
    dma = pltpu.SemaphoreType.DMA
    out = pl.pallas_call(
        kernel,
        out_shape=jax.ShapeDtypeStruct((3, 2 * OWN, 8, 128), f32),
        in_specs=[pl.BlockSpec(memory_space=pltpu.HBM), pl.BlockSpec(memory_space=pltpu.HBM)],
        out_specs=pl.BlockSpec(memory_space=pl.ANY),
        scratch_shapes=[pltpu.VMEM((2 * OWN, 8, 128), f32)] + [work] * 6 + [
            pltpu.VMEM((3, 2 * OWN, 8, 128), f32),
            pltpu.VMEM((GROUPS, RING, 3, 8, 128), f32),
            pltpu.VMEM((GROUPS, 3, 8, 128), f32),
            pltpu.VMEM((GROUPS, ROWS, 3, 8, 128), f32),
            pltpu.VMEM((GROUPS, RING, 3, 8, 128), f32),
            dma((2,)), dma((2, 2)), dma((2, 2)), dma((GROUPS,)), dma((GROUPS,)),
            dma((GROUPS, ROWS)), dma((GROUPS, ROWS)), dma((GROUPS, RING)), dma((GROUPS, RING)), dma((GROUPS,)),
        ],
        compiler_params=pltpu.CompilerParams(collective_id=0, has_side_effects=True, vmem_limit_bytes=32 * 1024 * 1024),
    )(pltpu.with_memory_space_constraint(states.reshape(3, 2 * OWN, 8, 128), pltpu.HBM), pltpu.with_memory_space_constraint(rate.reshape(2 * OWN, 8, 128), pltpu.HBM))
    return out.reshape(1, 3, OWN, 16, 128)


def solution(mesh):
    return jax.shard_map(
        shards,
        mesh=mesh,
        in_specs=(P("tm", None, "gz", None, None), P("gz", None, None)),
        out_specs=P("tm", None, "gz", None, None),
        check_vma=False,
    )
```
